512 devices in a mesh: tm: 256 (over z, y, x), state: 2 (over core).
Axes of the slice: x: 4, y: 4, z: 16, core: 2. Of those that a mesh axis runs over, the one named last changes fastest.
Arguments:
- diagonal: float32 [256, 512, 512], P('tm', None, 'state'), as said below
- lower: float32 [256, 512, 512], P('tm', None, 'state'), as said below
- rhs: float32 [256, 512, 128], P('tm', None, 'state'), may hold values from -6 to 6
Outputs:
- reduced_diagonal: float32 [256, 512, 512], P('tm', None, 'state')
- reduced_lower: float32 [256, 512, 512], P('tm', None, 'state')
- reduced_rhs: float32 [256, 512, 128], P('tm', None, 'state')
The draws below stay inside these ranges and needn't reach their ends.
Inputs may be any that keep to these rules, and one draw needn't show every extreme that they name: Every diagonal block is symmetric and positive definite, and the whole system is positive definite. `lower`: each coupling block is a full matrix; together with the diagonal blocks it forms the positive definite system.
All inputs are finite; a program needn't handle non-finite values.
Results may differ from the reference program's by a relative error of at most 0.0003.
Values sent between devices are 32-bit elements; how exact they have to be, the bound alone decides.
A program may use at most 64 MiB of HBM per device.

```python
import math
import jax
import jax.numpy as jnp
from jax import lax

S = 512
SEQS = 128
BLOCKS = 256


def transition(key, precision_low, precision_high):
    key_precision, key_retain, key_normal = jax.random.split(key, 3)
    precision = jnp.exp(jax.random.uniform(key_precision, (BLOCKS, S), jnp.float32, math.log(precision_low), math.log(precision_high)))
    retention = jax.random.uniform(key_retain, (BLOCKS, S), jnp.float32, 0.5, 0.95)
    mixing = jax.random.normal(key_normal, (BLOCKS, S, S), jnp.float32)
    identity = jnp.eye(S, dtype=jnp.float32)
    dynamics = retention[:, :, None] * identity[None, :, :] + 0.25 / math.sqrt(S) * mixing
    return (precision, dynamics)


def draw_lower(key, part):
    precision, dynamics = transition(key, 0.2, 20.0)
    return -precision[:, :, None] * dynamics


def draw_diagonal(key, part):
    precision, dynamics = transition(key, 0.2, 20.0)
    key = jax.random.fold_in(key, 11)
    key_scale, key_factor = jax.random.split(key)
    scales = jnp.exp(jax.random.uniform(key_scale, (BLOCKS, S), jnp.float32, math.log(0.05), math.log(5.0)))
    factor = jax.random.normal(key_factor, (BLOCKS, S, S), jnp.float32)
    ahead_precision = jnp.roll(precision, -1, axis=0)
    ahead_dynamics = jnp.roll(dynamics, -1, axis=0)
    identity = jnp.eye(S, dtype=jnp.float32)

    def one_block(items):
        own_precision, next_precision, next_dynamics, factor_one, scale_one = items
        carried = jnp.dot(next_dynamics.T * next_precision[None, :], next_dynamics, precision=lax.Precision.HIGHEST)
        measured = jnp.dot(factor_one * scale_one[None, :], factor_one.T, precision=lax.Precision.HIGHEST) * (1.0 / S)
        total = carried + measured
        total = (total + total.T) * 0.5
        return total + (own_precision + 0.1)[:, None] * identity
    return lax.map(one_block, (precision, ahead_precision, ahead_dynamics, factor, scales))


def steps_of(own_key, shape, shards, low, top_value):
    level, own = 1.0, jax.random.fold_in(own_key, 6)
    for axis_at, parts in shards:
        steps = jnp.exp(jax.random.uniform(jax.random.fold_in(own, axis_at), (parts,), jnp.float32, low / len(shards), top_value / len(shards)))
        level = level * jnp.repeat(steps, shape[axis_at] // parts).reshape([-1 if axis == axis_at else 1 for axis in range(len(shape))])
    return level


def centred(key, dims, spread, most, shards=(), kind=jnp.bfloat16):
    drawn = jax.random.normal(key, dims, jnp.float32) * spread
    if len(shards) > 0:
        drawn = steps_of(key, dims, shards, -0.22, 0.18) * drawn
    return jnp.clip(drawn, min=-most, max=most).astype(kind)


def setup_inputs(seed: int = 0) -> dict:
    keys = jax.random.split(jax.random.key(seed), 4)
    return {
        "diagonal": draw_diagonal(jax.random.fold_in(keys[3], 71), 0),
        "lower": draw_lower(jax.random.fold_in(keys[3], 71), 0),
        "rhs": centred(keys[2], (BLOCKS, S, SEQS), 1.0, 6.0, ((0, 256), (2, 2)), jnp.float32),
    }


def reduce_level(diag, low, rhs, stride):
    blocks = diag.shape[0]
    size = diag.shape[1]
    zeros_square = jnp.zeros((stride, size, size), diag.dtype)
    low_next = jnp.concatenate([low[stride:], zeros_square], axis=0)

    def one_block(items):
        diag_one, low_one, next_one, rhs_one = items
        factor = jnp.linalg.cholesky(diag_one)
        stacked = jnp.concatenate([next_one.T, low_one, rhs_one], axis=1)
        solved = jax.scipy.linalg.cho_solve((factor, True), stacked)
        upward = jnp.dot(next_one, solved, precision=lax.Precision.HIGHEST)
        downward = jnp.dot(low_one.T, solved[:, size:], precision=lax.Precision.HIGHEST)
        return (upward, downward)
    upward, downward = lax.map(one_block, (diag, low, low_next, rhs))
    zeros_up = jnp.zeros((stride,) + upward.shape[1:], upward.dtype)
    zeros_down = jnp.zeros((stride,) + downward.shape[1:], downward.dtype)
    below = jnp.concatenate([zeros_up, upward[:blocks - stride]], axis=0)
    above = jnp.concatenate([downward[stride:], zeros_down], axis=0)
    new_diag = diag - below[:, :, :size] - above[:, :, :size]
    new_low = -below[:, :, size:2 * size]
    new_rhs = rhs - below[:, :, 2 * size:] - above[:, :, size:]
    return (new_diag, new_low, new_rhs)

def reference(diagonal, lower, rhs):
    blocks = diagonal.shape[0]
    keep = (jnp.arange(blocks) > 0).astype(lower.dtype)
    low = lower * keep[:, None, None]
    diag = diagonal
    vectors = rhs
    for stride in (1, 2):
        diag, low, vectors = reduce_level(diag, low, vectors, stride)
    return (diag, low, vectors)
```

```python
import functools

import jax
import jax.numpy as jnp
from jax import lax
from jax.experimental import pallas as pl
from jax.experimental.pallas import tpu as pltpu
from jax.sharding import PartitionSpec as P

MESH = pl.DeviceIdType.MESH
F32 = jnp.float32
BF16 = jnp.bfloat16
VMEM = pltpu.VMEM
VMEM_LIMIT = 24 * 1024 * 1024

NN = (((1,), (0,)), ((), ()))
NT = (((1,), (1,)), ((), ()))
TN = (((0,), (0,)), ((), ()))

TOLERANCE = 4e-3
MAX_STEPS = 30


def halves(x):
    high = x.astype(BF16)
    return high, (x - high.astype(F32)).astype(BF16)


def dot1(a, b, dims=NN):
    return lax.dot_general(a, b, dims, preferred_element_type=F32)


def dot3(a, b, dims=NN):
    return dot1(a[0], b[0], dims) + (dot1(a[0], b[1], dims) + dot1(a[1], b[0], dims))


def neighbours(stride):
    length = lax.axis_size("tm")
    row = lax.axis_index("tm")
    core = lax.axis_index("state")
    up = (lax.rem(row + stride, length), core)
    down = (lax.rem(row + length - stride, length), core)
    return row, core, up, down, (row, 1 - core)


def greet(devices):
    barrier = pltpu.get_barrier_semaphore()
    for device in devices:
        pl.semaphore_signal(barrier, inc=1, device_id=device, device_id_type=MESH)
    pl.semaphore_wait(barrier, len(devices))


def send(src, dst, sems, at, device):
    copy = pltpu.make_async_remote_copy(
        src_ref=src,
        dst_ref=dst,
        send_sem=sems.at[0, at],
        recv_sem=sems.at[1, at],
        device_id=device,
        device_id_type=MESH,
    )
    copy.start()
    return copy


def join_kernel(part_ref, full_ref, sems, local_sem):
    _, core, _, _, sibling = neighbours(1)
    width = part_ref.shape[1]
    mine = full_ref.at[:, pl.ds(pl.multiple_of(core * width, width), width)]
    greet((sibling,))
    across = send(part_ref, mine, sems, 0, sibling)
    local = pltpu.make_async_copy(part_ref, mine, local_sem)
    local.start()
    across.wait()
    local.wait()


def join(part):
    size, width = part.shape
    return pl.pallas_call(
        join_kernel,
        out_shape=jax.ShapeDtypeStruct((size, 2 * width), F32),
        in_specs=[pl.BlockSpec(memory_space=pltpu.HBM)],
        out_specs=pl.BlockSpec(memory_space=VMEM),
        scratch_shapes=[pltpu.SemaphoreType.DMA((2, 1)), pltpu.SemaphoreType.DMA],
        compiler_params=pltpu.CompilerParams(
            collective_id=0, has_side_effects=True, vmem_limit_bytes=VMEM_LIMIT
        ),
        name="join_halves",
    )(part)


def invert_kernel(d_ref, p_ref, x_ref, a_high, a_low):
    size = d_ref.shape[0]
    rows = lax.broadcasted_iota(jnp.int32, (size, size), 0)
    cols = lax.broadcasted_iota(jnp.int32, (size, size), 1)
    eye = (rows == cols).astype(F32)
    diag = d_ref[...] * eye
    scale_row = lax.rsqrt(jnp.sum(diag, axis=0, keepdims=True))
    scale_col = lax.rsqrt(jnp.sum(diag, axis=1, keepdims=True))

    def scaled():
        return d_ref[...] * scale_col * scale_row

    a = scaled()
    high, low = halves(a)
    a_high[...] = high
    a_low[...] = low
    off = a - eye
    off_high = off.astype(BF16)
    square = dot1(off_high, off_high)
    top = 1.0 + jnp.sqrt(jnp.sqrt(jnp.sum(square * square))) * 1.01
    bottom = top * (1.0 / 12.0)
    ratio = (top - bottom) / (top + bottom)
    spread = ratio * ratio / (2.0 - ratio * ratio)
    half_sum = 0.5 * (top + bottom)
    gain = 2.0 / (2.0 - ratio * ratio)
    alpha = 2.0 * gain / half_sum
    beta = -gain / (half_sum * half_sum)
    x = (alpha + beta) * eye + beta * off
    resid = (1.0 - alpha - beta) * eye - (alpha + 2.0 * beta) * off - beta * square
    gain = 2.0 / (2.0 - spread * spread)
    x = gain * (x + dot1(x.astype(BF16), resid.astype(BF16)))
    spread = spread * spread / (2.0 - spread * spread)
    gain = 2.0 / (2.0 - spread * spread)
    x_high = x.astype(BF16)
    resid = eye - dot1(a_high[...], x_high)
    x_ref[...] = gain * (x + dot1(x_high, resid.astype(BF16)))

    def going(state):
        step, norm = state
        return jnp.logical_and(step < MAX_STEPS, norm >= TOLERANCE * TOLERANCE)

    def newton(state):
        step, _ = state
        x = x_ref[...]
        x_parts = halves(x)
        resid = eye - dot3((a_high[...], a_low[...]), x_parts)
        x_ref[...] = x + dot1(x_parts[0], resid.astype(BF16))
        return step + 1, jnp.sum(resid * resid)

    _, norm = lax.while_loop(going, newton, (jnp.int32(0), jnp.float32(1.0)))
    converged = norm < TOLERANCE * TOLERANCE

    @pl.when(jnp.logical_not(converged))
    def _():
        x_ref[...] = scaled()

        def eliminate(k, carry):
            block = x_ref[...]
            row = x_ref[pl.ds(k, 1), :]
            lane = lax.broadcasted_iota(jnp.int32, (1, size), 1) == k
            pivot = jnp.sum(jnp.where(lane, row, 0.0), axis=1, keepdims=True)
            row = jnp.where(lane, 1.0, row) / pivot
            column = jnp.sum(jnp.where(lane, block, 0.0), axis=1, keepdims=True)
            x_ref[...] = jnp.where(lane, 0.0, block) - column * row
            x_ref[pl.ds(k, 1), :] = row
            return carry

        lax.fori_loop(0, size, eliminate, 0)

    p_ref[...] = x_ref[...] * scale_col * scale_row


def invert(diag):
    size = diag.shape[0]
    return pl.pallas_call(
        invert_kernel,
        out_shape=jax.ShapeDtypeStruct((size, size), F32),
        in_specs=[pl.BlockSpec(memory_space=VMEM)],
        out_specs=pl.BlockSpec(memory_space=VMEM),
        scratch_shapes=[
            VMEM((size, size), F32),
            VMEM((size, size), BF16),
            VMEM((size, size), BF16),
        ],
        cost_estimate=pl.CostEstimate(
            flops=24 * size**3, bytes_accessed=8 * size * size, transcendentals=0
        ),
        compiler_params=pltpu.CompilerParams(vmem_limit_bytes=VMEM_LIMIT),
        name="invert_block",
    )(diag)


BLOCK = 128
PIECES = 5


def piece(ref, first_row, core, k):
    own, other = 2 * core, 2 - 2 * core
    row = (0, 0, 1, core, 1)[k]
    col = (own, own + 1, own + 1, other, other + core)[k]
    row = pl.multiple_of(first_row + row * BLOCK, BLOCK)
    col = pl.multiple_of(col * BLOCK, BLOCK)
    return ref.at[pl.ds(row, BLOCK), pl.ds(col, BLOCK)]


PLACES = (((0, 0), (0, 1), (1, 1), (0, 2), (1, 2)), ((2, 2), (2, 3), (3, 3), (3, 0), (3, 1)))


def unpack(pieces, full):
    for core in range(2):
        for k in range(PIECES):
            row, col = PLACES[core][k]
            value = pieces[core, k]
            full[row * BLOCK : (row + 1) * BLOCK, col * BLOCK : (col + 1) * BLOCK] = value
            if row != col:
                full[col * BLOCK : (col + 1) * BLOCK, row * BLOCK : (row + 1) * BLOCK] = value.T


def level_kernel(stride, last, *refs):
    ins = 4 if last else 5
    p_ref, low_ref, diag_ref, rhs_ref = refs[:4]
    diag_out, rhs_out, product_out = refs[ins : ins + 3]
    low_full, p_in, p_full, t_own, t_in, t_full, t_rhs_in, rhs_in, sems = refs[ins + 3 :]
    length = lax.axis_size("tm")
    row, core, up, down, sibling = neighbours(stride)
    size, width = low_ref.shape
    first = pl.multiple_of(core * width, width)
    mine = pl.ds(first, width)
    has_up = has_above = row + stride < length
    has_down = has_below = row >= stride

    barrier = pltpu.get_barrier_semaphore()

    def signal(device):
        pl.semaphore_signal(barrier, inc=1, device_id=device, device_id_type=MESH)

    signal(sibling)
    pl.when(has_up)(lambda: signal(up))
    pl.when(has_down)(lambda: signal(down))
    low_full[:, mine] = low_ref[...]
    pl.semaphore_wait(
        barrier, 1 + has_up.astype(jnp.int32) + has_down.astype(jnp.int32)
    )

    def copy(src, dst, at, device):
        return pltpu.make_async_remote_copy(
            src_ref=src,
            dst_ref=dst,
            send_sem=sems.at[0, at],
            recv_sem=sems.at[1, at],
            device_id=device,
            device_id_type=MESH,
        )

    p_up = [copy(piece(p_ref, first, core, k), p_in.at[core, k], k, up) for k in range(PIECES)]
    p_across = [
        copy(p_in.at[core, k], p_in.at[core, k], PIECES + k, sibling) for k in range(PIECES)
    ]
    t_down = [
        copy(piece(t_own, 0, core, k), t_in.at[core, k], 2 * PIECES + k, down)
        for k in range(PIECES)
    ]
    t_across = [
        copy(t_in.at[core, k], t_in.at[core, k], 3 * PIECES + k, sibling) for k in range(PIECES)
    ]
    rhs_up = copy(rhs_ref, rhs_in, 4 * PIECES, up)
    t_rhs_down = copy(t_own.at[width:], t_rhs_in, 4 * PIECES + 1, down)
    low_across = copy(low_ref, low_full.at[:, mine], 4 * PIECES + 2, sibling)

    def each(copies, call):
        for one in copies:
            getattr(one, call)()

    low_across.start()
    pl.when(has_up)(lambda: each(p_up + [rhs_up], "start"))
    own = halves(jnp.concatenate([low_ref[...].T, rhs_ref[...]], axis=0))
    own = halves(dot3(own, halves(p_ref[...])))
    low_across.wait()
    low = halves(low_full[...])
    t_own[...] = dot3(own, low)
    pl.when(has_down)(lambda: each(t_down + [t_rhs_down], "start"))

    @pl.when(has_below)
    def _():
        for k in range(PIECES):
            p_up[k].wait_recv()
            p_across[k].start()
        each(p_across, "wait_recv")

    unpack(p_in, p_full)
    carried = dot3(low, halves(p_full[...]))
    if last:
        product_out[...] = carried
    carried = halves(carried)
    from_diag = dot3(carried, low, NT)
    rest = diag_ref[...] - jnp.where(has_below, from_diag, 0.0)
    if not last:
        from_low = dot3(carried, halves(refs[4][...]))
        product_out[...] = jnp.where(row >= 2 * stride, -from_low, 0.0)
    pl.when(has_below)(rhs_up.wait_recv)
    from_rhs = dot3(halves(rhs_in[...]), carried, NT)

    @pl.when(has_above)
    def _():
        for k in range(PIECES):
            t_down[k].wait_recv()
            t_across[k].start()
        each(t_across, "wait_recv")

    unpack(t_in, t_full)
    if last:
        t_full[...] = rest - jnp.where(has_above, t_full[...], 0.0)
        diag_out[...] = t_full[:, mine]
    else:
        diag_out[...] = rest - jnp.where(has_above, t_full[...], 0.0)
    pl.when(has_above)(t_rhs_down.wait_recv)
    rhs_out[...] = (
        rhs_ref[...]
        - jnp.where(has_below, from_rhs, 0.0)
        - jnp.where(has_above, t_rhs_in[...], 0.0)
    )
    pl.when(has_up)(lambda: each(p_up + [rhs_up], "wait_send"))
    pl.when(has_down)(lambda: each(t_down + [t_rhs_down], "wait_send"))
    pl.when(has_below)(lambda: each(p_across, "wait_send"))
    pl.when(has_above)(lambda: each(t_across, "wait_send"))


def level(stride, p, low_cols, diag, rhs, low_prev=None):
    last = low_prev is None
    size, width = low_cols.shape
    seqs = rhs.shape[0]
    full = jax.ShapeDtypeStruct((size, size), F32)
    half = jax.ShapeDtypeStruct((size, width), F32)
    pieces = VMEM((2, PIECES, BLOCK, BLOCK), F32)
    ins = (p, low_cols, diag, rhs) + (() if last else (low_prev,))
    return pl.pallas_call(
        functools.partial(level_kernel, stride, last),
        out_shape=(
            half if last else full,
            jax.ShapeDtypeStruct((seqs, size), F32),
            full if last else half,
        ),
        in_specs=[pl.BlockSpec(memory_space=VMEM)] * len(ins),
        out_specs=[pl.BlockSpec(memory_space=VMEM)] * 3,
        scratch_shapes=[
            VMEM((size, size), F32),
            pieces,
            VMEM((size, size), F32),
            VMEM((width + seqs, size), F32),
            pieces,
            VMEM((size, size), F32),
            VMEM((seqs, size), F32),
            VMEM((seqs, size), F32),
            pltpu.SemaphoreType.DMA((2, 4 * PIECES + 3)),
        ],
        compiler_params=pltpu.CompilerParams(
            collective_id=stride, has_side_effects=True, vmem_limit_bytes=VMEM_LIMIT
        ),
        name="level_%d" % stride,
    )(*ins)


def finish_kernel(stride, carried_ref, low_prev_ref, diag_ref, rhs_ref, diag_out, low_out, rhs_out):
    product = dot3(halves(carried_ref[...]), halves(low_prev_ref[...]))
    low_out[...] = jnp.where(lax.axis_index("tm") >= 2 * stride, -product, 0.0)
    diag_out[...] = diag_ref[...]
    rhs_out[...] = rhs_ref[...]


def finish(stride, carried, low_prev, diag, rhs):
    half = jax.ShapeDtypeStruct(diag.shape, F32)
    return pl.pallas_call(
        functools.partial(finish_kernel, stride),
        out_shape=(half, half, jax.ShapeDtypeStruct(rhs.shape, F32)),
        in_specs=[pl.BlockSpec(memory_space=VMEM)] * 4,
        out_specs=[pl.BlockSpec(memory_space=VMEM)] * 3,
        compiler_params=pltpu.CompilerParams(vmem_limit_bytes=VMEM_LIMIT),
        name="finish",
    )(carried, low_prev, diag, rhs)


def passed_up(array, stride):
    length = lax.axis_size("tm")
    return lax.ppermute(array, "tm", [(i, i + stride) for i in range(length - stride)])


def per_device(diagonal, lower, rhs):
    low_cols, rhs_rows = lower[0], rhs[0].T
    low_prev = passed_up(low_cols, 1)
    diag = join(diagonal[0])
    diag, rhs_rows, low_cols = level(1, invert(diag), low_cols, diag, rhs_rows, low_prev)
    low_prev = passed_up(low_cols, 2)
    diag, rhs_rows, carried = level(2, invert(diag), low_cols, diag, rhs_rows)
    diag, low_cols, rhs_rows = finish(2, carried, low_prev, diag, rhs_rows)
    return diag[None], low_cols[None], rhs_rows.T[None]


def solution(mesh):
    placed = (P("tm", None, "state"),) * 3
    return jax.shard_map(
        per_device, mesh=mesh, in_specs=placed, out_specs=placed, check_vma=False
    )
```

```python
import functools

import jax
import jax.numpy as jnp
from jax import lax
from jax.experimental import pallas as pl
from jax.experimental.pallas import tpu as pltpu
from jax.sharding import PartitionSpec as P

MESH = pl.DeviceIdType.MESH
F32 = jnp.float32
BF16 = jnp.bfloat16
VMEM = pltpu.VMEM
VMEM_LIMIT = 24 * 1024 * 1024

NN = (((1,), (0,)), ((), ()))
NT = (((1,), (1,)), ((), ()))
TN = (((0,), (0,)), ((), ()))

TOLERANCE = 6e-5
MAX_STEPS = 20


def halves(x):
    high = x.astype(BF16)
    return high, (x - high.astype(F32)).astype(BF16)


def dot1(a, b, dims=NN):
    return lax.dot_general(a, b, dims, preferred_element_type=F32)


def dot3(a, b, dims=NN):
    return dot1(a[0], b[0], dims) + (dot1(a[0], b[1], dims) + dot1(a[1], b[0], dims))


def neighbours(stride):
    length = lax.axis_size("tm")
    row = lax.axis_index("tm")
    core = lax.axis_index("state")
    up = (lax.rem(row + stride, length), core)
    down = (lax.rem(row + length - stride, length), core)
    return row, core, up, down, (row, 1 - core)


def greet(devices):
    barrier = pltpu.get_barrier_semaphore()
    for device in devices:
        pl.semaphore_signal(barrier, inc=1, device_id=device, device_id_type=MESH)
    pl.semaphore_wait(barrier, len(devices))


def send(src, dst, sems, at, device):
    copy = pltpu.make_async_remote_copy(
        src_ref=src,
        dst_ref=dst,
        send_sem=sems.at[0, at],
        recv_sem=sems.at[1, at],
        device_id=device,
        device_id_type=MESH,
    )
    copy.start()
    return copy


def join_kernel(part_ref, full_ref, sems, local_sem):
    _, core, _, _, sibling = neighbours(1)
    width = part_ref.shape[1]
    mine = full_ref.at[:, pl.ds(pl.multiple_of(core * width, width), width)]
    greet((sibling,))
    across = send(part_ref, mine, sems, 0, sibling)
    local = pltpu.make_async_copy(part_ref, mine, local_sem)
    local.start()
    across.wait()
    local.wait()


def join(part):
    size, width = part.shape
    return pl.pallas_call(
        join_kernel,
        out_shape=jax.ShapeDtypeStruct((size, 2 * width), F32),
        in_specs=[pl.BlockSpec(memory_space=pltpu.HBM)],
        out_specs=pl.BlockSpec(memory_space=VMEM),
        scratch_shapes=[pltpu.SemaphoreType.DMA((2, 1)), pltpu.SemaphoreType.DMA],
        compiler_params=pltpu.CompilerParams(
            collective_id=0, has_side_effects=True, vmem_limit_bytes=VMEM_LIMIT
        ),
        name="join_halves",
    )(part)


def invert_kernel(d_ref, p_ref, inverse_ref, x_ref, a_high, a_low):
    size = d_ref.shape[0]
    rows = lax.broadcasted_iota(jnp.int32, (size, size), 0)
    cols = lax.broadcasted_iota(jnp.int32, (size, size), 1)
    eye = (rows == cols).astype(F32)
    diag = d_ref[...] * eye
    scale_row = lax.rsqrt(jnp.sum(diag, axis=0, keepdims=True))
    scale_col = lax.rsqrt(jnp.sum(diag, axis=1, keepdims=True))

    def scaled():
        return d_ref[...] * scale_col * scale_row

    a = scaled()
    high, low = halves(a)
    a_high[...] = high
    a_low[...] = low
    off = a - eye
    off_high = off.astype(BF16)
    square = dot1(off_high, off_high)
    top = 1.0 + jnp.sqrt(jnp.sqrt(jnp.sum(square * square))) * 1.01
    bottom = top * (1.0 / 12.0)
    ratio = (top - bottom) / (top + bottom)
    spread = ratio * ratio / (2.0 - ratio * ratio)
    half_sum = 0.5 * (top + bottom)
    gain = 2.0 / (2.0 - ratio * ratio)
    alpha = 2.0 * gain / half_sum
    beta = -gain / (half_sum * half_sum)
    x = (alpha + beta) * eye + beta * off
    resid = (1.0 - alpha - beta) * eye - (alpha + 2.0 * beta) * off - beta * square
    gain = 2.0 / (2.0 - spread * spread)
    x = gain * (x + dot1(x.astype(BF16), resid.astype(BF16)))
    spread = spread * spread / (2.0 - spread * spread)
    gain = 2.0 / (2.0 - spread * spread)
    x_high = x.astype(BF16)
    resid = eye - dot1(a_high[...], x_high)
    x_ref[...] = (gain * (x + dot1(x_high, resid.astype(BF16)))).astype(BF16)

    def refine(state):
        step, _ = state
        x = x_ref[...]
        resid = eye - (dot1(a_high[...], x) + dot1(a_low[...], x))
        resid_high = resid.astype(BF16)
        second = dot1(resid_high, resid_high)
        bound = jnp.sum(resid * resid) * jnp.sum(second * second)
        change = halves(resid + second)
        new = x.astype(F32) + (dot1(x, change[0]) + dot1(x, change[1]))
        x_ref[...] = new.astype(BF16)
        inverse_ref[...] = new
        return step + 1, bound

    limit = TOLERANCE * TOLERANCE * size

    def going(state):
        step, bound = state
        return jnp.logical_and(step < MAX_STEPS, bound >= limit)

    _, bound = lax.while_loop(going, refine, refine((jnp.int32(0), jnp.float32(0.0))))
    converged = bound < limit

    @pl.when(jnp.logical_not(converged))
    def _():
        inverse_ref[...] = scaled()

        def eliminate(k, carry):
            block = inverse_ref[...]
            row = inverse_ref[pl.ds(k, 1), :]
            lane = lax.broadcasted_iota(jnp.int32, (1, size), 1) == k
            pivot = jnp.sum(jnp.where(lane, row, 0.0), axis=1, keepdims=True)
            row = jnp.where(lane, 1.0, row) / pivot
            column = jnp.sum(jnp.where(lane, block, 0.0), axis=1, keepdims=True)
            inverse_ref[...] = jnp.where(lane, 0.0, block) - column * row
            inverse_ref[pl.ds(k, 1), :] = row
            return carry

        lax.fori_loop(0, size, eliminate, 0)

    p_ref[...] = inverse_ref[...] * scale_col * scale_row


def invert(diag):
    size = diag.shape[0]
    return pl.pallas_call(
        invert_kernel,
        out_shape=jax.ShapeDtypeStruct((size, size), F32),
        in_specs=[pl.BlockSpec(memory_space=VMEM)],
        out_specs=pl.BlockSpec(memory_space=VMEM),
        scratch_shapes=[
            VMEM((size, size), F32),
            VMEM((size, size), BF16),
            VMEM((size, size), BF16),
            VMEM((size, size), BF16),
        ],
        cost_estimate=pl.CostEstimate(
            flops=24 * size**3, bytes_accessed=8 * size * size, transcendentals=0
        ),
        compiler_params=pltpu.CompilerParams(vmem_limit_bytes=VMEM_LIMIT),
        name="invert_block",
    )(diag)


BLOCK = 128
PIECES = 5


def piece(ref, first_row, core, k):
    own, other = 2 * core, 2 - 2 * core
    row = (0, 0, 1, core, 1)[k]
    col = (own, own + 1, own + 1, other, other + core)[k]
    row = pl.multiple_of(first_row + row * BLOCK, BLOCK)
    col = pl.multiple_of(col * BLOCK, BLOCK)
    return ref.at[pl.ds(row, BLOCK), pl.ds(col, BLOCK)]


PLACES = (((0, 0), (0, 1), (1, 1), (0, 2), (1, 2)), ((2, 2), (2, 3), (3, 3), (3, 0), (3, 1)))


def unpack(pieces, full):
    for core in range(2):
        for k in range(PIECES):
            row, col = PLACES[core][k]
            value = pieces[core, k]
            full[row * BLOCK : (row + 1) * BLOCK, col * BLOCK : (col + 1) * BLOCK] = value
            if row != col:
                full[col * BLOCK : (col + 1) * BLOCK, row * BLOCK : (row + 1) * BLOCK] = value.T


def level_kernel(
    stride, last, p_ref, low_ref, diag_ref, rhs_ref, diag_out, rhs_out, carried_out,
    low_full, p_in, p_full, t_own, t_in, t_full, t_rhs_in, rhs_in, *rest,
):
    relay = stride > 1
    if relay:
        p_relay, t_relay, rhs_relay, t_rhs_relay, sems = rest
    else:
        (sems,) = rest
    length = lax.axis_size("tm")
    row, core, up, down, sibling = neighbours(1)
    size, width = low_ref.shape
    first = pl.multiple_of(core * width, width)
    mine = pl.ds(first, width)
    has_up = has_above = row + stride < length
    has_down = has_below = row >= stride
    near_up, near_down = row + 1 < length, row >= 1
    between = jnp.logical_and(near_up, near_down)

    barrier = pltpu.get_barrier_semaphore()

    def signal(device):
        pl.semaphore_signal(barrier, inc=1, device_id=device, device_id_type=MESH)

    signal(sibling)
    pl.when(near_up)(lambda: signal(up))
    pl.when(near_down)(lambda: signal(down))
    low_full[:, mine] = low_ref[...]
    pl.semaphore_wait(
        barrier, 1 + near_up.astype(jnp.int32) + near_down.astype(jnp.int32)
    )

    used = iter(range(sems.shape[1]))

    def copy(src, dst, device):
        at = next(used)
        return pltpu.make_async_remote_copy(
            src_ref=src,
            dst_ref=dst,
            send_sem=sems.at[0, at],
            recv_sem=sems.at[1, at],
            device_id=device,
            device_id_type=MESH,
        )

    def path(src, held, dst, device):
        if not relay:
            return [copy(src, dst, device)]
        return [copy(src, held, device), copy(held, dst, device)]

    p_paths = [
        path(piece(p_ref, first, core, k), relay and p_relay.at[k], p_in.at[core, k], up)
        for k in range(PIECES)
    ]
    t_paths = [
        path(piece(t_own, 0, core, k), relay and t_relay.at[k], t_in.at[core, k], down)
        for k in range(PIECES)
    ]
    p_paths.append(path(rhs_ref, relay and rhs_relay, rhs_in, up))
    t_paths.append(path(t_own.at[width:], relay and t_rhs_relay, t_rhs_in, down))
    p_across = [copy(p_in.at[core, k], p_in.at[core, k], sibling) for k in range(PIECES)]
    t_across = [copy(t_in.at[core, k], t_in.at[core, k], sibling) for k in range(PIECES)]
    low_across = copy(low_ref, low_full.at[:, mine], sibling)

    def each(copies, call):
        for one in copies:
            getattr(one, call)()

    low_across.start()
    pl.when(has_up)(lambda: each([way[0] for way in p_paths], "start"))
    own = halves(jnp.concatenate([low_ref[...].T, rhs_ref[...]], axis=0))
    own = halves(dot3(own, halves(p_ref[...])))
    low_across.wait()
    low = halves(low_full[...])
    t_own[...] = dot3(own, low)
    pl.when(has_down)(lambda: each([way[0] for way in t_paths], "start"))

    if relay:

        @pl.when(between)
        def _():
            order = p_paths[:3]
            for k in range(3):
                order += [t_paths[k], p_paths[3 + k]]
            for way in order + t_paths[3:]:
                way[0].wait_recv()
                way[1].start()

    @pl.when(has_below)
    def _():
        for k in range(PIECES):
            p_paths[k][-1].wait_recv()
            p_across[k].start()
        each(p_across, "wait_recv")

    unpack(p_in, p_full)
    carried = dot3(low, halves(p_full[...]))
    carried_out[...] = carried
    carried = halves(carried)
    from_diag = dot3(carried, low, NT)
    left = diag_ref[...] - jnp.where(has_below, from_diag, 0.0)
    pl.when(has_below)(p_paths[PIECES][-1].wait_recv)
    from_rhs = dot3(halves(rhs_in[...]), carried, NT)

    @pl.when(has_above)
    def _():
        for k in range(PIECES):
            t_paths[k][-1].wait_recv()
            t_across[k].start()
        each(t_across, "wait_recv")

    unpack(t_in, t_full)
    if last:
        t_full[...] = left - jnp.where(has_above, t_full[...], 0.0)
        diag_out[...] = t_full[:, mine]
    else:
        diag_out[...] = left - jnp.where(has_above, t_full[...], 0.0)
    pl.when(has_above)(t_paths[PIECES][-1].wait_recv)
    rhs_out[...] = (
        rhs_ref[...]
        - jnp.where(has_below, from_rhs, 0.0)
        - jnp.where(has_above, t_rhs_in[...], 0.0)
    )
    pl.when(has_up)(lambda: each([way[0] for way in p_paths], "wait_send"))
    pl.when(has_down)(lambda: each([way[0] for way in t_paths], "wait_send"))
    if relay:
        pl.when(between)(lambda: each([way[1] for way in p_paths + t_paths], "wait_send"))
    pl.when(has_below)(lambda: each(p_across, "wait_send"))
    pl.when(has_above)(lambda: each(t_across, "wait_send"))


def level(stride, last, p, low_cols, diag, rhs):
    size, width = low_cols.shape
    seqs = rhs.shape[0]
    full = jax.ShapeDtypeStruct((size, size), F32)
    half = jax.ShapeDtypeStruct((size, width), F32)
    pieces = VMEM((2, PIECES, BLOCK, BLOCK), F32)
    vectors = VMEM((seqs, size), F32)
    relays = [VMEM((PIECES, BLOCK, BLOCK), F32)] * 2 + [vectors] * 2
    copies = 4 * PIECES + 3 + (2 * PIECES + 2) * (stride > 1)
    return pl.pallas_call(
        functools.partial(level_kernel, stride, last),
        out_shape=(half if last else full, jax.ShapeDtypeStruct((seqs, size), F32), full),
        in_specs=[pl.BlockSpec(memory_space=VMEM)] * 4,
        out_specs=[pl.BlockSpec(memory_space=VMEM)] * 3,
        scratch_shapes=[
            VMEM((size, size), F32),
            pieces,
            VMEM((size, size), F32),
            VMEM((width + seqs, size), F32),
            pieces,
            VMEM((size, size), F32),
            vectors,
            vectors,
            *(relays if stride > 1 else ()),
            pltpu.SemaphoreType.DMA((2, copies)),
        ],
        compiler_params=pltpu.CompilerParams(
            collective_id=stride, has_side_effects=True, vmem_limit_bytes=VMEM_LIMIT
        ),
        name="level_%d" % stride,
    )(p, low_cols, diag, rhs)


def couple_kernel(stride, carried_ref, low_prev_ref, low_out):
    product = dot3(halves(carried_ref[...]), halves(low_prev_ref[...]))
    low_out[...] = jnp.where(lax.axis_index("tm") >= 2 * stride, -product, 0.0)


def couple(stride, carried, low_prev):
    return pl.pallas_call(
        functools.partial(couple_kernel, stride),
        out_shape=jax.ShapeDtypeStruct(low_prev.shape, F32),
        in_specs=[pl.BlockSpec(memory_space=VMEM)] * 2,
        out_specs=pl.BlockSpec(memory_space=VMEM),
        compiler_params=pltpu.CompilerParams(vmem_limit_bytes=VMEM_LIMIT),
        name="couple",
    )(carried, low_prev)


def finish_kernel(stride, carried_ref, low_prev_ref, diag_ref, rhs_ref, diag_out, low_out, rhs_out):
    couple_kernel(stride, carried_ref, low_prev_ref, low_out)
    diag_out[...] = diag_ref[...]
    rhs_out[...] = rhs_ref[...]


def finish(stride, carried, low_prev, diag, rhs):
    half = jax.ShapeDtypeStruct(diag.shape, F32)
    return pl.pallas_call(
        functools.partial(finish_kernel, stride),
        out_shape=(half, half, jax.ShapeDtypeStruct(rhs.shape, F32)),
        in_specs=[pl.BlockSpec(memory_space=VMEM)] * 4,
        out_specs=[pl.BlockSpec(memory_space=VMEM)] * 3,
        compiler_params=pltpu.CompilerParams(vmem_limit_bytes=VMEM_LIMIT),
        name="finish",
    )(carried, low_prev, diag, rhs)


def passed_up(array, stride):
    length = lax.axis_size("tm")
    return lax.ppermute(array, "tm", [(i, i + stride) for i in range(length - stride)])


def per_device(diagonal, lower, rhs):
    low_cols, rhs_rows = lower[0], rhs[0].T
    low_prev = passed_up(low_cols, 1)
    diag = join(diagonal[0])
    diag, rhs_rows, carried = level(1, False, invert(diag), low_cols, diag, rhs_rows)
    low_cols = couple(1, carried, low_prev)
    low_prev = passed_up(low_cols, 2)
    diag, rhs_rows, carried = level(2, True, invert(diag), low_cols, diag, rhs_rows)
    diag, low_cols, rhs_rows = finish(2, carried, low_prev, diag, rhs_rows)
    return diag[None], low_cols[None], rhs_rows.T[None]


def solution(mesh):
    placed = (P("tm", None, "state"),) * 3
    return jax.shard_map(
        per_device, mesh=mesh, in_specs=placed, out_specs=placed, check_vma=False
    )
```

```python
import functools

import jax
import jax.numpy as jnp
from jax import lax
from jax.experimental import pallas as pl
from jax.experimental.pallas import tpu as pltpu
from jax.sharding import PartitionSpec as P

MESH = pl.DeviceIdType.MESH
F32 = jnp.float32
BF16 = jnp.bfloat16
VMEM = pltpu.VMEM
VMEM_LIMIT = 24 * 1024 * 1024

NN = (((1,), (0,)), ((), ()))
NT = (((1,), (1,)), ((), ()))
TN = (((0,), (0,)), ((), ()))

TOLERANCE = 6e-5
MAX_STEPS = 20


def halves(x):
    high = x.astype(BF16)
    return high, (x - high.astype(F32)).astype(BF16)


def dot1(a, b, dims=NN):
    return lax.dot_general(a, b, dims, preferred_element_type=F32)


def dot3(a, b, dims=NN):
    return dot1(a[0], b[0], dims) + (dot1(a[0], b[1], dims) + dot1(a[1], b[0], dims))


def neighbours(stride):
    length = lax.axis_size("tm")
    row = lax.axis_index("tm")
    core = lax.axis_index("state")
    up = (lax.rem(row + stride, length), core)
    down = (lax.rem(row + length - stride, length), core)
    return row, core, up, down, (row, 1 - core)


def greet(devices):
    barrier = pltpu.get_barrier_semaphore()
    for device in devices:
        pl.semaphore_signal(barrier, inc=1, device_id=device, device_id_type=MESH)
    pl.semaphore_wait(barrier, len(devices))


def send(src, dst, sems, at, device):
    copy = pltpu.make_async_remote_copy(
        src_ref=src,
        dst_ref=dst,
        send_sem=sems.at[0, at],
        recv_sem=sems.at[1, at],
        device_id=device,
        device_id_type=MESH,
    )
    copy.start()
    return copy


def join_kernel(part_ref, full_ref, sems, local_sem):
    _, core, _, _, sibling = neighbours(1)
    width = part_ref.shape[1]
    mine = full_ref.at[:, pl.ds(pl.multiple_of(core * width, width), width)]
    greet((sibling,))
    across = send(part_ref, mine, sems, 0, sibling)
    local = pltpu.make_async_copy(part_ref, mine, local_sem)
    local.start()
    across.wait()
    local.wait()


def join(part):
    size, width = part.shape
    return pl.pallas_call(
        join_kernel,
        out_shape=jax.ShapeDtypeStruct((size, 2 * width), F32),
        in_specs=[pl.BlockSpec(memory_space=pltpu.HBM)],
        out_specs=pl.BlockSpec(memory_space=VMEM),
        scratch_shapes=[pltpu.SemaphoreType.DMA((2, 1)), pltpu.SemaphoreType.DMA],
        compiler_params=pltpu.CompilerParams(
            collective_id=0, has_side_effects=True, vmem_limit_bytes=VMEM_LIMIT
        ),
        name="join_halves",
    )(part)


def invert_kernel(d_ref, p_ref, inverse_ref, x_ref, a_high, a_low):
    size = d_ref.shape[0]
    rows = lax.broadcasted_iota(jnp.int32, (size, size), 0)
    cols = lax.broadcasted_iota(jnp.int32, (size, size), 1)
    eye = (rows == cols).astype(F32)
    diag = d_ref[...] * eye
    scale_row = lax.rsqrt(jnp.sum(diag, axis=0, keepdims=True))
    scale_col = lax.rsqrt(jnp.sum(diag, axis=1, keepdims=True))

    def scaled():
        return d_ref[...] * scale_col * scale_row

    a = scaled()
    high, low = halves(a)
    a_high[...] = high
    a_low[...] = low
    off = a - eye
    off_high = off.astype(BF16)
    square = dot1(off_high, off_high)
    top = 1.0 + jnp.sqrt(jnp.sqrt(jnp.sum(square * square))) * 1.01
    bottom = top * (1.0 / 12.0)
    ratio = (top - bottom) / (top + bottom)
    spread = ratio * ratio / (2.0 - ratio * ratio)
    half_sum = 0.5 * (top + bottom)
    gain = 2.0 / (2.0 - ratio * ratio)
    alpha = 2.0 * gain / half_sum
    beta = -gain / (half_sum * half_sum)
    x = (alpha + beta) * eye + beta * off
    resid = (1.0 - alpha - beta) * eye - (alpha + 2.0 * beta) * off - beta * square
    gain = 2.0 / (2.0 - spread * spread)
    x = gain * (x + dot1(x.astype(BF16), resid.astype(BF16)))
    spread = spread * spread / (2.0 - spread * spread)
    gain = 2.0 / (2.0 - spread * spread)
    x_high = x.astype(BF16)
    resid = eye - dot1(a_high[...], x_high)
    x_ref[...] = (gain * (x + dot1(x_high, resid.astype(BF16)))).astype(BF16)

    def refine(state):
        step, _ = state
        x = x_ref[...]
        resid = eye - (dot1(a_high[...], x) + dot1(a_low[...], x))
        resid_high = resid.astype(BF16)
        second = dot1(resid_high, resid_high)
        bound = jnp.sum(resid * resid) * jnp.sum(second * second)
        change = halves(resid + second)
        new = x.astype(F32) + (dot1(x, change[0]) + dot1(x, change[1]))
        x_ref[...] = new.astype(BF16)
        inverse_ref[...] = new
        return step + 1, bound

    limit = TOLERANCE * TOLERANCE * size

    def going(state):
        step, bound = state
        return jnp.logical_and(step < MAX_STEPS, bound >= limit)

    _, bound = lax.while_loop(going, refine, refine((jnp.int32(0), jnp.float32(0.0))))
    converged = bound < limit

    @pl.when(jnp.logical_not(converged))
    def _():
        inverse_ref[...] = scaled()

        def eliminate(k, carry):
            block = inverse_ref[...]
            row = inverse_ref[pl.ds(k, 1), :]
            lane = lax.broadcasted_iota(jnp.int32, (1, size), 1) == k
            pivot = jnp.sum(jnp.where(lane, row, 0.0), axis=1, keepdims=True)
            row = jnp.where(lane, 1.0, row) / pivot
            column = jnp.sum(jnp.where(lane, block, 0.0), axis=1, keepdims=True)
            inverse_ref[...] = jnp.where(lane, 0.0, block) - column * row
            inverse_ref[pl.ds(k, 1), :] = row
            return carry

        lax.fori_loop(0, size, eliminate, 0)

    p_ref[...] = inverse_ref[...] * scale_col * scale_row


def invert(diag):
    size = diag.shape[0]
    return pl.pallas_call(
        invert_kernel,
        out_shape=jax.ShapeDtypeStruct((size, size), F32),
        in_specs=[pl.BlockSpec(memory_space=VMEM)],
        out_specs=pl.BlockSpec(memory_space=VMEM),
        scratch_shapes=[
            VMEM((size, size), F32),
            VMEM((size, size), BF16),
            VMEM((size, size), BF16),
            VMEM((size, size), BF16),
        ],
        cost_estimate=pl.CostEstimate(
            flops=24 * size**3, bytes_accessed=8 * size * size, transcendentals=0
        ),
        compiler_params=pltpu.CompilerParams(vmem_limit_bytes=VMEM_LIMIT),
        name="invert_block",
    )(diag)


BLOCK = 128
PACKED = 4 * BLOCK + 8
CHUNKS = ((0, 2 * BLOCK), (2 * BLOCK, 2 * BLOCK + 8))


def pack(ref, first_row, core, packed):
    own, other = 2 * core, 2 - 2 * core

    def block(row, col):
        row = pl.multiple_of(first_row + row * BLOCK, BLOCK)
        col = pl.multiple_of(col * BLOCK, BLOCK)
        return ref[pl.ds(row, BLOCK), pl.ds(col, BLOCK)]

    packed[:BLOCK] = block(0, own + 1)
    packed[BLOCK : 2 * BLOCK] = block(core, other)
    packed[2 * BLOCK : 3 * BLOCK] = block(1, other + core)
    rows = lax.broadcasted_iota(jnp.int32, (BLOCK, BLOCK), 0)
    cols = lax.broadcasted_iota(jnp.int32, (BLOCK, BLOCK), 1)
    second = block(1, own + 1)
    packed[3 * BLOCK : 4 * BLOCK] = jnp.where(rows >= cols, block(0, own), second)
    diagonal = jnp.sum(jnp.where(rows == cols, second, 0.0), axis=0, keepdims=True)
    packed[4 * BLOCK :] = jnp.broadcast_to(diagonal, (8, BLOCK))


def unpack(shares, full):
    def put(row, col, value):
        full[row * BLOCK : (row + 1) * BLOCK, col * BLOCK : (col + 1) * BLOCK] = value

    rows = lax.broadcasted_iota(jnp.int32, (BLOCK, BLOCK), 0)
    cols = lax.broadcasted_iota(jnp.int32, (BLOCK, BLOCK), 1)
    for core, places in enumerate((((0, 1), (0, 2), (1, 2)), ((2, 3), (3, 0), (3, 1)))):
        for k, (row, col) in enumerate(places):
            value = shares[core, k * BLOCK : (k + 1) * BLOCK]
            put(row, col, value)
            put(col, row, value.T)
        both = shares[core, 3 * BLOCK : 4 * BLOCK]
        turned = both.T
        diagonal = shares[core, 4 * BLOCK : 4 * BLOCK + 1]
        put(2 * core, 2 * core, jnp.where(rows >= cols, both, turned))
        second = jnp.where(rows < cols, both, jnp.where(rows > cols, turned, diagonal))
        put(2 * core + 1, 2 * core + 1, second)


def level_kernel(
    stride, last, p_ref, low_ref, diag_ref, rhs_ref, diag_out, rhs_out, carried_out,
    low_full, p_out, p_in, p_full, t_own, t_out, t_in, t_full, t_rhs_in, rhs_in, *rest,
):
    relay = stride > 1
    if relay:
        p_relay, t_relay, rhs_relay, t_rhs_relay, sems = rest
    else:
        (sems,) = rest
    length = lax.axis_size("tm")
    row, core, up, down, sibling = neighbours(1)
    size, width = low_ref.shape
    first = pl.multiple_of(core * width, width)
    mine = pl.ds(first, width)
    has_up = has_above = row + stride < length
    has_down = has_below = row >= stride
    near_up, near_down = row + 1 < length, row >= 1
    between = jnp.logical_and(near_up, near_down)

    barrier = pltpu.get_barrier_semaphore()

    def signal(device):
        pl.semaphore_signal(barrier, inc=1, device_id=device, device_id_type=MESH)

    signal(sibling)
    pl.when(near_up)(lambda: signal(up))
    pl.when(near_down)(lambda: signal(down))
    low_full[:, mine] = low_ref[...]
    pack(p_ref, first, core, p_out)
    pl.semaphore_wait(
        barrier, 1 + near_up.astype(jnp.int32) + near_down.astype(jnp.int32)
    )

    used = iter(range(sems.shape[1]))

    def copy(src, dst, device):
        at = next(used)
        return pltpu.make_async_remote_copy(
            src_ref=src,
            dst_ref=dst,
            send_sem=sems.at[0, at],
            recv_sem=sems.at[1, at],
            device_id=device,
            device_id_type=MESH,
        )

    def path(src, held, dst, device):
        if not relay:
            return [copy(src, dst, device)]
        return [copy(src, held, device), copy(held, dst, device)]

    def packed_paths(out, held, into, device):
        return [
            path(out.at[pl.ds(at, n)], relay and held.at[pl.ds(at, n)], into.at[core, pl.ds(at, n)], device)
            for at, n in CHUNKS
        ]

    def packed_across(into):
        parts = [into.at[core, pl.ds(at, n)] for at, n in CHUNKS]
        return [copy(part, part, sibling) for part in parts]

    p_paths = packed_paths(p_out, relay and p_relay, p_in, up)
    t_paths = packed_paths(t_out, relay and t_relay, t_in, down)
    p_paths.append(path(rhs_ref, relay and rhs_relay, rhs_in, up))
    t_paths.append(path(t_own.at[width:], relay and t_rhs_relay, t_rhs_in, down))
    p_across, t_across = packed_across(p_in), packed_across(t_in)
    low_across = copy(low_ref, low_full.at[:, mine], sibling)

    def each(copies, call):
        for one in copies:
            getattr(one, call)()

    low_across.start()
    pl.when(has_up)(lambda: each([way[0] for way in p_paths], "start"))
    own = halves(jnp.concatenate([low_ref[...].T, rhs_ref[...]], axis=0))
    own = halves(dot3(own, halves(p_ref[...])))
    low_across.wait()
    low = halves(low_full[...])
    t_own[...] = dot3(own, low)
    pack(t_own, 0, core, t_out)
    pl.when(has_down)(lambda: each([way[0] for way in t_paths], "start"))

    if relay:

        @pl.when(between)
        def _():
            for way in p_paths[:2] + t_paths[:1] + p_paths[2:] + t_paths[1:]:
                way[0].wait_recv()
                way[1].start()

    @pl.when(has_below)
    def _():
        for way, across in zip(p_paths, p_across):
            way[-1].wait_recv()
            across.start()
        each(p_across, "wait_recv")

    unpack(p_in, p_full)
    carried = dot3(low, halves(p_full[...]))
    carried_out[...] = carried
    carried = halves(carried)
    from_diag = dot3(carried, low, NT)
    left = diag_ref[...] - jnp.where(has_below, from_diag, 0.0)
    pl.when(has_below)(p_paths[-1][-1].wait_recv)
    from_rhs = dot3(halves(rhs_in[...]), carried, NT)

    @pl.when(has_above)
    def _():
        for way, across in zip(t_paths, t_across):
            way[-1].wait_recv()
            across.start()
        each(t_across, "wait_recv")

    unpack(t_in, t_full)
    if last:
        t_full[...] = left - jnp.where(has_above, t_full[...], 0.0)
        diag_out[...] = t_full[:, mine]
    else:
        diag_out[...] = left - jnp.where(has_above, t_full[...], 0.0)
    pl.when(has_above)(t_paths[-1][-1].wait_recv)
    rhs_out[...] = (
        rhs_ref[...]
        - jnp.where(has_below, from_rhs, 0.0)
        - jnp.where(has_above, t_rhs_in[...], 0.0)
    )
    pl.when(has_up)(lambda: each([way[0] for way in p_paths], "wait_send"))
    pl.when(has_down)(lambda: each([way[0] for way in t_paths], "wait_send"))
    if relay:
        pl.when(between)(lambda: each([way[1] for way in p_paths + t_paths], "wait_send"))
    pl.when(has_below)(lambda: each(p_across, "wait_send"))
    pl.when(has_above)(lambda: each(t_across, "wait_send"))


def level(stride, last, p, low_cols, diag, rhs):
    size, width = low_cols.shape
    seqs = rhs.shape[0]
    full = jax.ShapeDtypeStruct((size, size), F32)
    half = jax.ShapeDtypeStruct((size, width), F32)
    share = VMEM((PACKED, BLOCK), F32)
    shares = VMEM((2, PACKED, BLOCK), F32)
    vectors = VMEM((seqs, size), F32)
    relays = [share, share, vectors, vectors]
    copies = 4 * len(CHUNKS) + 3 + (2 * len(CHUNKS) + 2) * (stride > 1)
    return pl.pallas_call(
        functools.partial(level_kernel, stride, last),
        out_shape=(half if last else full, jax.ShapeDtypeStruct((seqs, size), F32), full),
        in_specs=[pl.BlockSpec(memory_space=VMEM)] * 4,
        out_specs=[pl.BlockSpec(memory_space=VMEM)] * 3,
        scratch_shapes=[
            VMEM((size, size), F32),
            share,
            shares,
            VMEM((size, size), F32),
            VMEM((width + seqs, size), F32),
            share,
            shares,
            VMEM((size, size), F32),
            vectors,
            vectors,
            *(relays if stride > 1 else ()),
            pltpu.SemaphoreType.DMA((2, copies)),
        ],
        compiler_params=pltpu.CompilerParams(
            collective_id=stride, has_side_effects=True, vmem_limit_bytes=VMEM_LIMIT
        ),
        name="level_%d" % stride,
    )(p, low_cols, diag, rhs)


def couple_kernel(stride, carried_ref, low_prev_ref, low_out):
    product = dot3(halves(carried_ref[...]), halves(low_prev_ref[...]))
    low_out[...] = jnp.where(lax.axis_index("tm") >= 2 * stride, -product, 0.0)


def couple(stride, carried, low_prev):
    return pl.pallas_call(
        functools.partial(couple_kernel, stride),
        out_shape=jax.ShapeDtypeStruct(low_prev.shape, F32),
        in_specs=[pl.BlockSpec(memory_space=VMEM)] * 2,
        out_specs=pl.BlockSpec(memory_space=VMEM),
        compiler_params=pltpu.CompilerParams(vmem_limit_bytes=VMEM_LIMIT),
        name="couple",
    )(carried, low_prev)


def finish_kernel(stride, carried_ref, low_prev_ref, diag_ref, rhs_ref, diag_out, low_out, rhs_out):
    couple_kernel(stride, carried_ref, low_prev_ref, low_out)
    diag_out[...] = diag_ref[...]
    rhs_out[...] = rhs_ref[...]


def finish(stride, carried, low_prev, diag, rhs):
    half = jax.ShapeDtypeStruct(diag.shape, F32)
    return pl.pallas_call(
        functools.partial(finish_kernel, stride),
        out_shape=(half, half, jax.ShapeDtypeStruct(rhs.shape, F32)),
        in_specs=[pl.BlockSpec(memory_space=VMEM)] * 4,
        out_specs=[pl.BlockSpec(memory_space=VMEM)] * 3,
        compiler_params=pltpu.CompilerParams(vmem_limit_bytes=VMEM_LIMIT),
        name="finish",
    )(carried, low_prev, diag, rhs)


def passed_up(array, stride):
    length = lax.axis_size("tm")
    return lax.ppermute(array, "tm", [(i, i + stride) for i in range(length - stride)])


def per_device(diagonal, lower, rhs):
    low_cols, rhs_rows = lower[0], rhs[0].T
    low_prev = passed_up(low_cols, 1)
    diag = join(diagonal[0])
    diag, rhs_rows, carried = level(1, False, invert(diag), low_cols, diag, rhs_rows)
    low_cols = couple(1, carried, low_prev)
    low_prev = passed_up(low_cols, 2)
    diag, rhs_rows, carried = level(2, True, invert(diag), low_cols, diag, rhs_rows)
    diag, low_cols, rhs_rows = finish(2, carried, low_prev, diag, rhs_rows)
    return diag[None], low_cols[None], rhs_rows.T[None]


def solution(mesh):
    placed = (P("tm", None, "state"),) * 3
    return jax.shard_map(
        per_device, mesh=mesh, in_specs=placed, out_specs=placed, check_vma=False
    )
```

```python
import functools

import jax
import jax.numpy as jnp
from jax import lax
from jax.experimental import pallas as pl
from jax.experimental.pallas import tpu as pltpu
from jax.sharding import PartitionSpec as P

MESH = pl.DeviceIdType.MESH
F32 = jnp.float32
BF16 = jnp.bfloat16
VMEM = pltpu.VMEM
VMEM_LIMIT = 24 * 1024 * 1024

NN = (((1,), (0,)), ((), ()))
NT = (((1,), (1,)), ((), ()))
TN = (((0,), (0,)), ((), ()))

TOLERANCE = 5e-5
MAX_STEPS = 20


def halves(x):
    high = x.astype(BF16)
    return high, (x - high.astype(F32)).astype(BF16)


def dot1(a, b, dims=NN):
    return lax.dot_general(a, b, dims, preferred_element_type=F32)


def dot3(a, b, dims=NN):
    return dot1(a[0], b[0], dims) + (dot1(a[0], b[1], dims) + dot1(a[1], b[0], dims))


def neighbours(stride):
    length = lax.axis_size("tm")
    row = lax.axis_index("tm")
    core = lax.axis_index("state")
    up = (lax.rem(row + stride, length), core)
    down = (lax.rem(row + length - stride, length), core)
    return row, core, up, down, (row, 1 - core)


def greet(devices):
    barrier = pltpu.get_barrier_semaphore()
    for device in devices:
        pl.semaphore_signal(barrier, inc=1, device_id=device, device_id_type=MESH)
    pl.semaphore_wait(barrier, len(devices))


def send(src, dst, sems, at, device):
    copy = pltpu.make_async_remote_copy(
        src_ref=src,
        dst_ref=dst,
        send_sem=sems.at[0, at],
        recv_sem=sems.at[1, at],
        device_id=device,
        device_id_type=MESH,
    )
    copy.start()
    return copy


def join_kernel(part_ref, full_ref, sems, local_sem):
    _, core, _, _, sibling = neighbours(1)
    width = part_ref.shape[1]
    mine = full_ref.at[:, pl.ds(pl.multiple_of(core * width, width), width)]
    greet((sibling,))
    across = send(part_ref, mine, sems, 0, sibling)
    local = pltpu.make_async_copy(part_ref, mine, local_sem)
    local.start()
    across.wait()
    local.wait()


def join(part):
    size, width = part.shape
    return pl.pallas_call(
        join_kernel,
        out_shape=jax.ShapeDtypeStruct((size, 2 * width), F32),
        in_specs=[pl.BlockSpec(memory_space=pltpu.HBM)],
        out_specs=pl.BlockSpec(memory_space=VMEM),
        scratch_shapes=[pltpu.SemaphoreType.DMA((2, 1)), pltpu.SemaphoreType.DMA],
        compiler_params=pltpu.CompilerParams(
            collective_id=0, has_side_effects=True, vmem_limit_bytes=VMEM_LIMIT
        ),
        name="join_halves",
    )(part)


def invert_kernel(d_ref, p_ref, inverse_ref, x_ref, a_high, a_low):
    size = d_ref.shape[0]
    rows = lax.broadcasted_iota(jnp.int32, (size, size), 0)
    cols = lax.broadcasted_iota(jnp.int32, (size, size), 1)
    eye = (rows == cols).astype(F32)
    diag = d_ref[...] * eye
    scale_row = lax.rsqrt(jnp.sum(diag, axis=0, keepdims=True))
    scale_col = lax.rsqrt(jnp.sum(diag, axis=1, keepdims=True))

    def scaled():
        return d_ref[...] * scale_col * scale_row

    a = scaled()
    high, low = halves(a)
    a_high[...] = high
    a_low[...] = low
    off = a - eye
    off_high = off.astype(BF16)
    square = dot1(off_high, off_high)
    top = 1.0 + jnp.sqrt(jnp.sqrt(jnp.sum(square * square))) * 1.01
    bottom = top * (1.0 / 12.0)
    ratio = (top - bottom) / (top + bottom)
    spread = ratio * ratio / (2.0 - ratio * ratio)
    half_sum = 0.5 * (top + bottom)
    gain = 2.0 / (2.0 - ratio * ratio)
    alpha = 2.0 * gain / half_sum
    beta = -gain / (half_sum * half_sum)
    x = (alpha + beta) * eye + beta * off
    resid = (1.0 - alpha - beta) * eye - (alpha + 2.0 * beta) * off - beta * square
    gain = 2.0 / (2.0 - spread * spread)
    x = gain * (x + dot1(x.astype(BF16), resid.astype(BF16)))
    spread = spread * spread / (2.0 - spread * spread)
    gain = 2.0 / (2.0 - spread * spread)
    x_high = x.astype(BF16)
    resid = eye - dot1(a_high[...], x_high)
    x_ref[...] = (gain * (x + dot1(x_high, resid.astype(BF16)))).astype(BF16)

    def refine(state):
        step, _ = state
        x = x_ref[...]
        resid = eye - (dot1(a_high[...], x) + dot1(a_low[...], x))
        resid_high = resid.astype(BF16)
        second = dot1(resid_high, resid_high)
        bound = jnp.sum(second * second)
        bound = bound * jnp.sqrt(bound)
        change = halves(resid + second)
        new = x.astype(F32) + (dot1(x, change[0]) + dot1(x, change[1]))
        x_ref[...] = new.astype(BF16)
        inverse_ref[...] = new
        return step + 1, bound

    limit = TOLERANCE * TOLERANCE * size

    def going(state):
        step, bound = state
        return jnp.logical_and(step < MAX_STEPS, bound >= limit)

    _, bound = lax.while_loop(going, refine, refine((jnp.int32(0), jnp.float32(0.0))))
    converged = bound < limit

    @pl.when(jnp.logical_not(converged))
    def _():
        inverse_ref[...] = scaled()

        def eliminate(k, carry):
            block = inverse_ref[...]
            row = inverse_ref[pl.ds(k, 1), :]
            lane = lax.broadcasted_iota(jnp.int32, (1, size), 1) == k
            pivot = jnp.sum(jnp.where(lane, row, 0.0), axis=1, keepdims=True)
            row = jnp.where(lane, 1.0, row) / pivot
            column = jnp.sum(jnp.where(lane, block, 0.0), axis=1, keepdims=True)
            inverse_ref[...] = jnp.where(lane, 0.0, block) - column * row
            inverse_ref[pl.ds(k, 1), :] = row
            return carry

        lax.fori_loop(0, size, eliminate, 0)

    p_ref[...] = inverse_ref[...] * scale_col * scale_row


def invert(diag):
    size = diag.shape[0]
    return pl.pallas_call(
        invert_kernel,
        out_shape=jax.ShapeDtypeStruct((size, size), F32),
        in_specs=[pl.BlockSpec(memory_space=VMEM)],
        out_specs=pl.BlockSpec(memory_space=VMEM),
        scratch_shapes=[
            VMEM((size, size), F32),
            VMEM((size, size), BF16),
            VMEM((size, size), BF16),
            VMEM((size, size), BF16),
        ],
        cost_estimate=pl.CostEstimate(
            flops=24 * size**3, bytes_accessed=8 * size * size, transcendentals=0
        ),
        compiler_params=pltpu.CompilerParams(vmem_limit_bytes=VMEM_LIMIT),
        name="invert_block",
    )(diag)


BLOCK = 128
PACKED = 4 * BLOCK + 8
CHUNKS = ((0, 2 * BLOCK), (2 * BLOCK, 2 * BLOCK + 8))


def pack(ref, first_row, core, packed):
    own, other = 2 * core, 2 - 2 * core

    def block(row, col):
        row = pl.multiple_of(first_row + row * BLOCK, BLOCK)
        col = pl.multiple_of(col * BLOCK, BLOCK)
        return ref[pl.ds(row, BLOCK), pl.ds(col, BLOCK)]

    packed[:BLOCK] = block(0, own + 1)
    packed[BLOCK : 2 * BLOCK] = block(core, other)
    packed[2 * BLOCK : 3 * BLOCK] = block(1, other + core)
    rows = lax.broadcasted_iota(jnp.int32, (BLOCK, BLOCK), 0)
    cols = lax.broadcasted_iota(jnp.int32, (BLOCK, BLOCK), 1)
    second = block(1, own + 1)
    packed[3 * BLOCK : 4 * BLOCK] = jnp.where(rows >= cols, block(0, own), second)
    diagonal = jnp.sum(jnp.where(rows == cols, second, 0.0), axis=0, keepdims=True)
    packed[4 * BLOCK :] = jnp.broadcast_to(diagonal, (8, BLOCK))


def unpack(shares, full):
    def put(row, col, value):
        full[row * BLOCK : (row + 1) * BLOCK, col * BLOCK : (col + 1) * BLOCK] = value

    rows = lax.broadcasted_iota(jnp.int32, (BLOCK, BLOCK), 0)
    cols = lax.broadcasted_iota(jnp.int32, (BLOCK, BLOCK), 1)
    for core, places in enumerate((((0, 1), (0, 2), (1, 2)), ((2, 3), (3, 0), (3, 1)))):
        for k, (row, col) in enumerate(places):
            value = shares[core, k * BLOCK : (k + 1) * BLOCK]
            put(row, col, value)
            put(col, row, value.T)
        both = shares[core, 3 * BLOCK : 4 * BLOCK]
        turned = both.T
        diagonal = shares[core, 4 * BLOCK : 4 * BLOCK + 1]
        put(2 * core, 2 * core, jnp.where(rows >= cols, both, turned))
        second = jnp.where(rows < cols, both, jnp.where(rows > cols, turned, diagonal))
        put(2 * core + 1, 2 * core + 1, second)


def level_kernel(
    stride, last, p_ref, low_ref, diag_ref, rhs_ref, diag_out, rhs_out, carried_out,
    low_full, p_out, p_in, p_full, t_own, t_out, t_in, t_full, t_rhs_in, rhs_in, *rest,
):
    relay = stride > 1
    if relay:
        p_relay, t_relay, rhs_relay, t_rhs_relay, sems = rest
    else:
        (sems,) = rest
    length = lax.axis_size("tm")
    row, core, up, down, sibling = neighbours(1)
    size, width = low_ref.shape
    first = pl.multiple_of(core * width, width)
    mine = pl.ds(first, width)
    has_up = has_above = row + stride < length
    has_down = has_below = row >= stride
    near_up, near_down = row + 1 < length, row >= 1
    between = jnp.logical_and(near_up, near_down)

    barrier = pltpu.get_barrier_semaphore()

    def signal(device):
        pl.semaphore_signal(barrier, inc=1, device_id=device, device_id_type=MESH)

    signal(sibling)
    pl.when(near_up)(lambda: signal(up))
    pl.when(near_down)(lambda: signal(down))
    low_full[:, mine] = low_ref[...]
    pack(p_ref, first, core, p_out)
    pl.semaphore_wait(
        barrier, 1 + near_up.astype(jnp.int32) + near_down.astype(jnp.int32)
    )

    used = iter(range(sems.shape[1]))

    def copy(src, dst, device):
        at = next(used)
        return pltpu.make_async_remote_copy(
            src_ref=src,
            dst_ref=dst,
            send_sem=sems.at[0, at],
            recv_sem=sems.at[1, at],
            device_id=device,
            device_id_type=MESH,
        )

    def path(src, held, dst, device):
        if not relay:
            return [copy(src, dst, device)]
        return [copy(src, held, device), copy(held, dst, device)]

    def packed_paths(out, held, into, device):
        return [
            path(out.at[pl.ds(at, n)], relay and held.at[pl.ds(at, n)], into.at[core, pl.ds(at, n)], device)
            for at, n in CHUNKS
        ]

    def packed_across(into):
        parts = [into.at[core, pl.ds(at, n)] for at, n in CHUNKS]
        return [copy(part, part, sibling) for part in parts]

    p_paths = packed_paths(p_out, relay and p_relay, p_in, up)
    t_paths = packed_paths(t_out, relay and t_relay, t_in, down)
    p_paths.append(path(rhs_ref, relay and rhs_relay, rhs_in, up))
    t_paths.append(path(t_own.at[width:], relay and t_rhs_relay, t_rhs_in, down))
    p_across, t_across = packed_across(p_in), packed_across(t_in)
    low_across = copy(low_ref, low_full.at[:, mine], sibling)

    def each(copies, call):
        for one in copies:
            getattr(one, call)()

    def pass_on(ways):
        @pl.when(between)
        def _():
            for way in ways:
                way[0].wait_recv()
                way[1].start()

    *p_parts, rhs_path = p_paths
    *t_parts, t_rhs_path = t_paths
    low_across.start()
    pl.when(has_up)(lambda: each([way[0] for way in p_parts], "start"))
    own = halves(jnp.concatenate([low_ref[...].T, rhs_ref[...]], axis=0))
    own = halves(dot3(own, halves(p_ref[...])))
    low_across.wait()
    low = halves(low_full[...])
    t_own[...] = dot3(own, low)
    pack(t_own, 0, core, t_out)
    pl.when(has_down)(lambda: each([way[0] for way in t_parts], "start"))
    if relay:
        pass_on(p_parts)
        pl.when(has_up)(rhs_path[0].start)
        pass_on(t_parts)
        pl.when(has_down)(t_rhs_path[0].start)
        pass_on([rhs_path])

    @pl.when(has_below)
    def _():
        for way, across in zip(p_parts, p_across):
            way[-1].wait_recv()
            across.start()
        each(p_across, "wait_recv")

    if not relay:
        pl.when(has_up)(rhs_path[0].start)
        pl.when(has_down)(t_rhs_path[0].start)
    unpack(p_in, p_full)
    carried = dot3(low, halves(p_full[...]))
    carried_out[...] = carried
    carried = halves(carried)
    from_diag = dot3(carried, low, NT)
    left = diag_ref[...] - jnp.where(has_below, from_diag, 0.0)
    if relay:
        pass_on([t_rhs_path])
    pl.when(has_below)(rhs_path[-1].wait_recv)
    from_rhs = dot3(halves(rhs_in[...]), carried, NT)

    @pl.when(has_above)
    def _():
        for way, across in zip(t_parts, t_across):
            way[-1].wait_recv()
            across.start()
        each(t_across, "wait_recv")

    unpack(t_in, t_full)
    if last:
        t_full[...] = left - jnp.where(has_above, t_full[...], 0.0)
        diag_out[...] = t_full[:, mine]
    else:
        diag_out[...] = left - jnp.where(has_above, t_full[...], 0.0)
    pl.when(has_above)(t_rhs_path[-1].wait_recv)
    rhs_out[...] = (
        rhs_ref[...]
        - jnp.where(has_below, from_rhs, 0.0)
        - jnp.where(has_above, t_rhs_in[...], 0.0)
    )
    pl.when(has_up)(lambda: each([way[0] for way in p_paths], "wait_send"))
    pl.when(has_down)(lambda: each([way[0] for way in t_paths], "wait_send"))
    if relay:
        pl.when(between)(lambda: each([way[1] for way in p_paths + t_paths], "wait_send"))
    pl.when(has_below)(lambda: each(p_across, "wait_send"))
    pl.when(has_above)(lambda: each(t_across, "wait_send"))


def level(stride, last, p, low_cols, diag, rhs):
    size, width = low_cols.shape
    seqs = rhs.shape[0]
    full = jax.ShapeDtypeStruct((size, size), F32)
    half = jax.ShapeDtypeStruct((size, width), F32)
    share = VMEM((PACKED, BLOCK), F32)
    shares = VMEM((2, PACKED, BLOCK), F32)
    vectors = VMEM((seqs, size), F32)
    relays = [share, share, vectors, vectors]
    copies = 4 * len(CHUNKS) + 3 + (2 * len(CHUNKS) + 2) * (stride > 1)
    return pl.pallas_call(
        functools.partial(level_kernel, stride, last),
        out_shape=(half if last else full, jax.ShapeDtypeStruct((seqs, size), F32), full),
        in_specs=[pl.BlockSpec(memory_space=VMEM)] * 4,
        out_specs=[pl.BlockSpec(memory_space=VMEM)] * 3,
        scratch_shapes=[
            VMEM((size, size), F32),
            share,
            shares,
            VMEM((size, size), F32),
            VMEM((width + seqs, size), F32),
            share,
            shares,
            VMEM((size, size), F32),
            vectors,
            vectors,
            *(relays if stride > 1 else ()),
            pltpu.SemaphoreType.DMA((2, copies)),
        ],
        compiler_params=pltpu.CompilerParams(
            collective_id=stride, has_side_effects=True, vmem_limit_bytes=VMEM_LIMIT
        ),
        name="level_%d" % stride,
    )(p, low_cols, diag, rhs)


def couple_kernel(stride, carried_ref, low_prev_ref, low_out):
    product = dot3(halves(carried_ref[...]), halves(low_prev_ref[...]))
    low_out[...] = jnp.where(lax.axis_index("tm") >= 2 * stride, -product, 0.0)


def couple(stride, carried, low_prev):
    return pl.pallas_call(
        functools.partial(couple_kernel, stride),
        out_shape=jax.ShapeDtypeStruct(low_prev.shape, F32),
        in_specs=[pl.BlockSpec(memory_space=VMEM)] * 2,
        out_specs=pl.BlockSpec(memory_space=VMEM),
        compiler_params=pltpu.CompilerParams(vmem_limit_bytes=VMEM_LIMIT),
        name="couple",
    )(carried, low_prev)


def finish_kernel(stride, carried_ref, low_prev_ref, diag_ref, rhs_ref, diag_out, low_out, rhs_out):
    couple_kernel(stride, carried_ref, low_prev_ref, low_out)
    diag_out[...] = diag_ref[...]
    rhs_out[...] = rhs_ref[...]


def finish(stride, carried, low_prev, diag, rhs):
    half = jax.ShapeDtypeStruct(diag.shape, F32)
    return pl.pallas_call(
        functools.partial(finish_kernel, stride),
        out_shape=(half, half, jax.ShapeDtypeStruct(rhs.shape, F32)),
        in_specs=[pl.BlockSpec(memory_space=VMEM)] * 4,
        out_specs=[pl.BlockSpec(memory_space=VMEM)] * 3,
        compiler_params=pltpu.CompilerParams(vmem_limit_bytes=VMEM_LIMIT),
        name="finish",
    )(carried, low_prev, diag, rhs)


def passed_up(array, stride):
    length = lax.axis_size("tm")
    return lax.ppermute(array, "tm", [(i, i + stride) for i in range(length - stride)])


def per_device(diagonal, lower, rhs):
    low_cols, rhs_rows = lower[0], rhs[0].T
    low_prev = passed_up(low_cols, 1)
    diag = join(diagonal[0])
    diag, rhs_rows, carried = level(1, False, invert(diag), low_cols, diag, rhs_rows)
    low_cols = couple(1, carried, low_prev)
    low_prev = passed_up(low_cols, 2)
    diag, rhs_rows, carried = level(2, True, invert(diag), low_cols, diag, rhs_rows)
    diag, low_cols, rhs_rows = finish(2, carried, low_prev, diag, rhs_rows)
    return diag[None], low_cols[None], rhs_rows.T[None]


def solution(mesh):
    placed = (P("tm", None, "state"),) * 3
    return jax.shard_map(
        per_device, mesh=mesh, in_specs=placed, out_specs=placed, check_vma=False
    )
```

```python
import functools

import jax
import jax.numpy as jnp
from jax import lax
from jax.experimental import pallas as pl
from jax.experimental.pallas import tpu as pltpu
from jax.sharding import PartitionSpec as P

MESH = pl.DeviceIdType.MESH
F32 = jnp.float32
BF16 = jnp.bfloat16
VMEM = pltpu.VMEM
VMEM_LIMIT = 24 * 1024 * 1024

NN = (((1,), (0,)), ((), ()))
NT = (((1,), (1,)), ((), ()))
TN = (((0,), (0,)), ((), ()))

TOLERANCE = 5e-5
MAX_STEPS = 20


def halves(x):
    high = x.astype(BF16)
    return high, (x - high.astype(F32)).astype(BF16)


def dot1(a, b, dims=NN):
    return lax.dot_general(a, b, dims, preferred_element_type=F32)


def dot3(a, b, dims=NN):
    return dot1(a[0], b[0], dims) + (dot1(a[0], b[1], dims) + dot1(a[1], b[0], dims))


def neighbours(stride):
    length = lax.axis_size("tm")
    row = lax.axis_index("tm")
    core = lax.axis_index("state")
    up = (lax.rem(row + stride, length), core)
    down = (lax.rem(row + length - stride, length), core)
    return row, core, up, down, (row, 1 - core)


def greet(devices):
    barrier = pltpu.get_barrier_semaphore()
    for device in devices:
        pl.semaphore_signal(barrier, inc=1, device_id=device, device_id_type=MESH)
    pl.semaphore_wait(barrier, len(devices))


def send(src, dst, sems, at, device):
    copy = pltpu.make_async_remote_copy(
        src_ref=src,
        dst_ref=dst,
        send_sem=sems.at[0, at],
        recv_sem=sems.at[1, at],
        device_id=device,
        device_id_type=MESH,
    )
    copy.start()
    return copy


def join_kernel(part_ref, full_ref, sems, local_sem):
    _, core, _, _, sibling = neighbours(1)
    width = part_ref.shape[1]
    mine = full_ref.at[:, pl.ds(pl.multiple_of(core * width, width), width)]
    greet((sibling,))
    across = send(part_ref, mine, sems, 0, sibling)
    local = pltpu.make_async_copy(part_ref, mine, local_sem)
    local.start()
    across.wait()
    local.wait()


def join(part):
    size, width = part.shape
    return pl.pallas_call(
        join_kernel,
        out_shape=jax.ShapeDtypeStruct((size, 2 * width), F32),
        in_specs=[pl.BlockSpec(memory_space=pltpu.HBM)],
        out_specs=pl.BlockSpec(memory_space=VMEM),
        scratch_shapes=[pltpu.SemaphoreType.DMA((2, 1)), pltpu.SemaphoreType.DMA],
        compiler_params=pltpu.CompilerParams(
            collective_id=0, has_side_effects=True, vmem_limit_bytes=VMEM_LIMIT
        ),
        name="join_halves",
    )(part)


def invert_kernel(d_ref, p_ref, inverse_ref, x_ref, a_high, a_low):
    size = d_ref.shape[0]
    rows = lax.broadcasted_iota(jnp.int32, (size, size), 0)
    cols = lax.broadcasted_iota(jnp.int32, (size, size), 1)
    eye = (rows == cols).astype(F32)
    diag = d_ref[...] * eye
    scale_row = lax.rsqrt(jnp.sum(diag, axis=0, keepdims=True))
    scale_col = lax.rsqrt(jnp.sum(diag, axis=1, keepdims=True))

    def scaled():
        return d_ref[...] * scale_col * scale_row

    a = scaled()
    high, low = halves(a)
    a_high[...] = high
    a_low[...] = low
    off = a - eye
    off_high = off.astype(BF16)
    square = dot1(off_high, off_high)
    top = 1.0 + jnp.sqrt(jnp.sqrt(jnp.sum(square * square))) * 1.01
    bottom = top * (1.0 / 12.0)
    ratio = (top - bottom) / (top + bottom)
    spread = ratio * ratio / (2.0 - ratio * ratio)
    half_sum = 0.5 * (top + bottom)
    gain = 2.0 / (2.0 - ratio * ratio)
    alpha = 2.0 * gain / half_sum
    beta = -gain / (half_sum * half_sum)
    x = (alpha + beta) * eye + beta * off
    resid = (1.0 - alpha - beta) * eye - (alpha + 2.0 * beta) * off - beta * square
    gain = 2.0 / (2.0 - spread * spread)
    x = gain * (x + dot1(x.astype(BF16), resid.astype(BF16)))
    spread = spread * spread / (2.0 - spread * spread)
    gain = 2.0 / (2.0 - spread * spread)
    x_high = x.astype(BF16)
    resid = eye - dot1(a_high[...], x_high)
    x_ref[...] = (gain * (x + dot1(x_high, resid.astype(BF16)))).astype(BF16)

    def refine(state):
        step, _ = state
        x = x_ref[...]
        resid = eye - (dot1(a_high[...], x) + dot1(a_low[...], x))
        resid_high = resid.astype(BF16)
        second = dot1(resid_high, resid_high)
        bound = jnp.sum(second * second)
        bound = bound * jnp.sqrt(bound)
        change = halves(resid + second)
        new = x.astype(F32) + (dot1(x, change[0]) + dot1(x, change[1]))
        x_ref[...] = new.astype(BF16)
        inverse_ref[...] = new
        return step + 1, bound

    limit = TOLERANCE * TOLERANCE * size

    def going(state):
        step, bound = state
        return jnp.logical_and(step < MAX_STEPS, bound >= limit)

    _, bound = lax.while_loop(going, refine, refine((jnp.int32(0), jnp.float32(0.0))))
    converged = bound < limit

    @pl.when(jnp.logical_not(converged))
    def _():
        inverse_ref[...] = scaled()

        def eliminate(k, carry):
            block = inverse_ref[...]
            row = inverse_ref[pl.ds(k, 1), :]
            lane = lax.broadcasted_iota(jnp.int32, (1, size), 1) == k
            pivot = jnp.sum(jnp.where(lane, row, 0.0), axis=1, keepdims=True)
            row = jnp.where(lane, 1.0, row) / pivot
            column = jnp.sum(jnp.where(lane, block, 0.0), axis=1, keepdims=True)
            inverse_ref[...] = jnp.where(lane, 0.0, block) - column * row
            inverse_ref[pl.ds(k, 1), :] = row
            return carry

        lax.fori_loop(0, size, eliminate, 0)

    p_ref[...] = inverse_ref[...] * scale_col * scale_row


def invert(diag):
    size = diag.shape[0]
    return pl.pallas_call(
        invert_kernel,
        out_shape=jax.ShapeDtypeStruct((size, size), F32),
        in_specs=[pl.BlockSpec(memory_space=VMEM)],
        out_specs=pl.BlockSpec(memory_space=VMEM),
        scratch_shapes=[
            VMEM((size, size), F32),
            VMEM((size, size), BF16),
            VMEM((size, size), BF16),
            VMEM((size, size), BF16),
        ],
        cost_estimate=pl.CostEstimate(
            flops=24 * size**3, bytes_accessed=8 * size * size, transcendentals=0
        ),
        compiler_params=pltpu.CompilerParams(vmem_limit_bytes=VMEM_LIMIT),
        name="invert_block",
    )(diag)


BLOCK = 128
PACKED = 4 * BLOCK + 8
NEAR = 2 * BLOCK + 8
CHUNKS = ((0, NEAR), (NEAR, 2 * BLOCK))


def block_at(ref, row, col):
    row, col = pl.multiple_of(row * BLOCK, BLOCK), pl.multiple_of(col * BLOCK, BLOCK)
    return ref[pl.ds(row, BLOCK), pl.ds(col, BLOCK)]


def pack_near(ref, first, core, packed):
    own = 2 * core
    packed[:BLOCK] = block_at(ref, first, own + 1)
    rows = lax.broadcasted_iota(jnp.int32, (BLOCK, BLOCK), 0)
    cols = lax.broadcasted_iota(jnp.int32, (BLOCK, BLOCK), 1)
    second = block_at(ref, first + 1, own + 1)
    packed[BLOCK : 2 * BLOCK] = jnp.where(rows >= cols, block_at(ref, first, own), second)
    diagonal = jnp.sum(jnp.where(rows == cols, second, 0.0), axis=0, keepdims=True)
    packed[2 * BLOCK : NEAR] = jnp.broadcast_to(diagonal, (8, BLOCK))


def pack_far(ref, first, core, packed):
    other = 2 - 2 * core
    packed[NEAR : NEAR + BLOCK] = block_at(ref, first + core, other)
    packed[NEAR + BLOCK :] = block_at(ref, first + 1, other + core)


def unpack(shares, full):
    def put(row, col, value):
        full[row * BLOCK : (row + 1) * BLOCK, col * BLOCK : (col + 1) * BLOCK] = value

    rows = lax.broadcasted_iota(jnp.int32, (BLOCK, BLOCK), 0)
    cols = lax.broadcasted_iota(jnp.int32, (BLOCK, BLOCK), 1)
    for core, places in enumerate((((0, 1), (0, 2), (1, 2)), ((2, 3), (3, 0), (3, 1)))):
        for at, (row, col) in zip((0, NEAR, NEAR + BLOCK), places):
            value = shares[core, at : at + BLOCK]
            put(row, col, value)
            put(col, row, value.T)
        both = shares[core, BLOCK : 2 * BLOCK]
        turned = both.T
        diagonal = shares[core, 2 * BLOCK : 2 * BLOCK + 1]
        put(2 * core, 2 * core, jnp.where(rows >= cols, both, turned))
        second = jnp.where(rows < cols, both, jnp.where(rows > cols, turned, diagonal))
        put(2 * core + 1, 2 * core + 1, second)


def level_kernel(
    stride, last, p_ref, low_ref, diag_ref, rhs_ref, diag_out, rhs_out, carried_out,
    low_full, p_out, p_in, p_full, t_own, t_out, t_in, t_full, t_rhs_in, rhs_in, *rest,
):
    relay = stride > 1
    if relay:
        p_relay, t_relay, rhs_relay, t_rhs_relay, sems = rest
    else:
        (sems,) = rest
    length = lax.axis_size("tm")
    row, core, up, down, sibling = neighbours(1)
    size, width = low_ref.shape
    first = pl.multiple_of(core * width, width)
    mine = pl.ds(first, width)
    has_up = has_above = row + stride < length
    has_down = has_below = row >= stride
    near_up, near_down = row + 1 < length, row >= 1
    between = jnp.logical_and(near_up, near_down)

    barrier = pltpu.get_barrier_semaphore()

    def signal(device):
        pl.semaphore_signal(barrier, inc=1, device_id=device, device_id_type=MESH)

    signal(sibling)
    pl.when(near_up)(lambda: signal(up))
    pl.when(near_down)(lambda: signal(down))
    low_full[:, mine] = low_ref[...]
    pack_near(p_ref, 2 * core, core, p_out)
    pack_far(p_ref, 2 * core, core, p_out)
    pl.semaphore_wait(
        barrier, 1 + near_up.astype(jnp.int32) + near_down.astype(jnp.int32)
    )

    used = iter(range(sems.shape[1]))

    def copy(src, dst, device):
        at = next(used)
        return pltpu.make_async_remote_copy(
            src_ref=src,
            dst_ref=dst,
            send_sem=sems.at[0, at],
            recv_sem=sems.at[1, at],
            device_id=device,
            device_id_type=MESH,
        )

    def path(src, held, dst, device):
        if not relay:
            return [copy(src, dst, device)]
        return [copy(src, held, device), copy(held, dst, device)]

    def packed_paths(out, held, into, device):
        parts = [pl.ds(at, n) for at, n in CHUNKS]
        return [
            path(out.at[part], relay and held.at[part], into.at[core, part], device)
            for part in parts
        ]

    def packed_across(into):
        parts = [into.at[core, pl.ds(at, n)] for at, n in CHUNKS]
        return [copy(part, part, sibling) for part in parts]

    p_paths = packed_paths(p_out, relay and p_relay, p_in, up)
    t_paths = packed_paths(t_out, relay and t_relay, t_in, down)
    p_paths.append(path(rhs_ref, relay and rhs_relay, rhs_in, up))
    t_paths.append(path(t_own.at[width:], relay and t_rhs_relay, t_rhs_in, down))
    p_across, t_across = packed_across(p_in), packed_across(t_in)
    low_across = copy(low_ref, low_full.at[:, mine], sibling)

    def each(copies, call):
        for one in copies:
            getattr(one, call)()

    low_across.start()
    pl.when(has_up)(lambda: each([way[0] for way in p_paths], "start"))
    own = halves(jnp.concatenate([low_ref[...].T, rhs_ref[...]], axis=0))
    own = halves(dot3(own, halves(p_ref[...])))
    t_own[:, mine] = dot3(own, halves(low_ref[...]))
    pack_near(t_own, 0, core, t_out)
    pl.when(has_down)(t_paths[0][0].start)
    low_across.wait()
    others = pl.ds(pl.multiple_of((1 - core) * width, width), width)
    t_own[:, others] = dot3(own, halves(low_full[:, others]))
    pack_far(t_own, 0, core, t_out)
    pl.when(has_down)(lambda: each([way[0] for way in t_paths[1:]], "start"))
    low = halves(low_full[...])
    if relay:

        @pl.when(between)
        def _():
            for way in p_paths[:2] + t_paths[:1] + p_paths[2:] + t_paths[1:]:
                way[0].wait_recv()
                way[1].start()

    @pl.when(has_below)
    def _():
        for way, across in zip(p_paths, p_across):
            way[-1].wait_recv()
            across.start()
        each(p_across, "wait_recv")

    unpack(p_in, p_full)
    carried = dot3(low, halves(p_full[...]))
    carried_out[...] = carried
    carried = halves(carried)
    from_diag = dot3(carried, low, NT)
    left = diag_ref[...] - jnp.where(has_below, from_diag, 0.0)
    pl.when(has_below)(p_paths[-1][-1].wait_recv)
    from_rhs = dot3(halves(rhs_in[...]), carried, NT)

    @pl.when(has_above)
    def _():
        for way, across in zip(t_paths, t_across):
            way[-1].wait_recv()
            across.start()
        each(t_across, "wait_recv")

    unpack(t_in, t_full)
    if last:
        t_full[...] = left - jnp.where(has_above, t_full[...], 0.0)
        diag_out[...] = t_full[:, mine]
    else:
        diag_out[...] = left - jnp.where(has_above, t_full[...], 0.0)
    pl.when(has_above)(t_paths[-1][-1].wait_recv)
    rhs_out[...] = (
        rhs_ref[...]
        - jnp.where(has_below, from_rhs, 0.0)
        - jnp.where(has_above, t_rhs_in[...], 0.0)
    )
    pl.when(has_up)(lambda: each([way[0] for way in p_paths], "wait_send"))
    pl.when(has_down)(lambda: each([way[0] for way in t_paths], "wait_send"))
    if relay:
        pl.when(between)(lambda: each([way[1] for way in p_paths + t_paths], "wait_send"))
    pl.when(has_below)(lambda: each(p_across, "wait_send"))
    pl.when(has_above)(lambda: each(t_across, "wait_send"))


def level(stride, last, p, low_cols, diag, rhs):
    size, width = low_cols.shape
    seqs = rhs.shape[0]
    full = jax.ShapeDtypeStruct((size, size), F32)
    half = jax.ShapeDtypeStruct((size, width), F32)
    share = VMEM((PACKED, BLOCK), F32)
    shares = VMEM((2, PACKED, BLOCK), F32)
    vectors = VMEM((seqs, size), F32)
    relays = [share, share, vectors, vectors]
    copies = 4 * len(CHUNKS) + 3 + (2 * len(CHUNKS) + 2) * (stride > 1)
    return pl.pallas_call(
        functools.partial(level_kernel, stride, last),
        out_shape=(half if last else full, jax.ShapeDtypeStruct((seqs, size), F32), full),
        in_specs=[pl.BlockSpec(memory_space=VMEM)] * 4,
        out_specs=[pl.BlockSpec(memory_space=VMEM)] * 3,
        scratch_shapes=[
            VMEM((size, size), F32),
            share,
            shares,
            VMEM((size, size), F32),
            VMEM((width + seqs, size), F32),
            share,
            shares,
            VMEM((size, size), F32),
            vectors,
            vectors,
            *(relays if stride > 1 else ()),
            pltpu.SemaphoreType.DMA((2, copies)),
        ],
        compiler_params=pltpu.CompilerParams(
            collective_id=stride, has_side_effects=True, vmem_limit_bytes=VMEM_LIMIT
        ),
        name="level_%d" % stride,
    )(p, low_cols, diag, rhs)


def couple_kernel(stride, carried_ref, low_prev_ref, low_out):
    product = dot3(halves(carried_ref[...]), halves(low_prev_ref[...]))
    low_out[...] = jnp.where(lax.axis_index("tm") >= 2 * stride, -product, 0.0)


def couple(stride, carried, low_prev):
    return pl.pallas_call(
        functools.partial(couple_kernel, stride),
        out_shape=jax.ShapeDtypeStruct(low_prev.shape, F32),
        in_specs=[pl.BlockSpec(memory_space=VMEM)] * 2,
        out_specs=pl.BlockSpec(memory_space=VMEM),
        compiler_params=pltpu.CompilerParams(vmem_limit_bytes=VMEM_LIMIT),
        name="couple",
    )(carried, low_prev)


def finish_kernel(stride, carried_ref, low_prev_ref, diag_ref, rhs_ref, diag_out, low_out, rhs_out):
    couple_kernel(stride, carried_ref, low_prev_ref, low_out)
    diag_out[...] = diag_ref[...]
    rhs_out[...] = rhs_ref[...]


def finish(stride, carried, low_prev, diag, rhs):
    half = jax.ShapeDtypeStruct(diag.shape, F32)
    return pl.pallas_call(
        functools.partial(finish_kernel, stride),
        out_shape=(half, half, jax.ShapeDtypeStruct(rhs.shape, F32)),
        in_specs=[pl.BlockSpec(memory_space=VMEM)] * 4,
        out_specs=[pl.BlockSpec(memory_space=VMEM)] * 3,
        compiler_params=pltpu.CompilerParams(vmem_limit_bytes=VMEM_LIMIT),
        name="finish",
    )(carried, low_prev, diag, rhs)


def passed_up(array, stride):
    length = lax.axis_size("tm")
    return lax.ppermute(array, "tm", [(i, i + stride) for i in range(length - stride)])


def per_device(diagonal, lower, rhs):
    low_cols, rhs_rows = lower[0], rhs[0].T
    low_prev = passed_up(low_cols, 1)
    diag = join(diagonal[0])
    diag, rhs_rows, carried = level(1, False, invert(diag), low_cols, diag, rhs_rows)
    low_cols = couple(1, carried, low_prev)
    low_prev = passed_up(low_cols, 2)
    diag, rhs_rows, carried = level(2, True, invert(diag), low_cols, diag, rhs_rows)
    diag, low_cols, rhs_rows = finish(2, carried, low_prev, diag, rhs_rows)
    return diag[None], low_cols[None], rhs_rows.T[None]


def solution(mesh):
    placed = (P("tm", None, "state"),) * 3
    return jax.shard_map(
        per_device, mesh=mesh, in_specs=placed, out_specs=placed, check_vma=False
    )
```

```python
import functools

import jax
import jax.numpy as jnp
from jax import lax
from jax.experimental import pallas as pl
from jax.experimental.pallas import tpu as pltpu
from jax.sharding import PartitionSpec as P

MESH = pl.DeviceIdType.MESH
F32 = jnp.float32
BF16 = jnp.bfloat16
VMEM = pltpu.VMEM
VMEM_LIMIT = 24 * 1024 * 1024

NN = (((1,), (0,)), ((), ()))
NT = (((1,), (1,)), ((), ()))
TN = (((0,), (0,)), ((), ()))

TOLERANCE = 5e-5
MAX_STEPS = 20


def halves(x):
    high = x.astype(BF16)
    return high, (x - high.astype(F32)).astype(BF16)


def dot1(a, b, dims=NN):
    return lax.dot_general(a, b, dims, preferred_element_type=F32)


def dot3(a, b, dims=NN):
    return dot1(a[0], b[0], dims) + (dot1(a[0], b[1], dims) + dot1(a[1], b[0], dims))


RING = 4


def row_at(row, turn):
    return row - row % RING + (row + turn) % RING


def neighbours(stride):
    length = lax.axis_size("tm")
    row = lax.axis_index("tm")
    core = lax.axis_index("state")
    up = (lax.rem(row + stride, length), core)
    down = (lax.rem(row + length - stride, length), core)
    return row, core, up, down, (row, 1 - core)


def greet(devices):
    barrier = pltpu.get_barrier_semaphore()
    for device in devices:
        pl.semaphore_signal(barrier, inc=1, device_id=device, device_id_type=MESH)
    pl.semaphore_wait(barrier, len(devices))


def send(src, dst, sems, at, device):
    copy = pltpu.make_async_remote_copy(
        src_ref=src,
        dst_ref=dst,
        send_sem=sems.at[0, at],
        recv_sem=sems.at[1, at],
        device_id=device,
        device_id_type=MESH,
    )
    copy.start()
    return copy


def join_kernel(part_ref, full_ref, sems, local_sem):
    _, core, _, _, sibling = neighbours(1)
    width = part_ref.shape[1]
    mine = full_ref.at[:, pl.ds(pl.multiple_of(core * width, width), width)]
    greet((sibling,))
    across = send(part_ref, mine, sems, 0, sibling)
    local = pltpu.make_async_copy(part_ref, mine, local_sem)
    local.start()
    across.wait()
    local.wait()


def join(part):
    size, width = part.shape
    return pl.pallas_call(
        join_kernel,
        out_shape=jax.ShapeDtypeStruct((size, 2 * width), F32),
        in_specs=[pl.BlockSpec(memory_space=pltpu.HBM)],
        out_specs=pl.BlockSpec(memory_space=VMEM),
        scratch_shapes=[pltpu.SemaphoreType.DMA((2, 1)), pltpu.SemaphoreType.DMA],
        compiler_params=pltpu.CompilerParams(
            collective_id=0, has_side_effects=True, vmem_limit_bytes=VMEM_LIMIT
        ),
        name="join_halves",
    )(part)


def invert_kernel(d_ref, p_ref, inverse_ref, x_ref, a_high, a_low):
    size = d_ref.shape[0]
    rows = lax.broadcasted_iota(jnp.int32, (size, size), 0)
    cols = lax.broadcasted_iota(jnp.int32, (size, size), 1)
    eye = (rows == cols).astype(F32)
    diag = d_ref[...] * eye
    scale_row = lax.rsqrt(jnp.sum(diag, axis=0, keepdims=True))
    scale_col = lax.rsqrt(jnp.sum(diag, axis=1, keepdims=True))

    def scaled():
        return d_ref[...] * scale_col * scale_row

    a = scaled()
    high, low = halves(a)
    a_high[...] = high
    a_low[...] = low
    off = a - eye
    off_high = off.astype(BF16)
    square = dot1(off_high, off_high)
    top = 1.0 + jnp.sqrt(jnp.sqrt(jnp.sum(square * square))) * 1.01
    bottom = top * (1.0 / 12.0)
    ratio = (top - bottom) / (top + bottom)
    spread = ratio * ratio / (2.0 - ratio * ratio)
    half_sum = 0.5 * (top + bottom)
    gain = 2.0 / (2.0 - ratio * ratio)
    alpha = 2.0 * gain / half_sum
    beta = -gain / (half_sum * half_sum)
    x = (alpha + beta) * eye + beta * off
    resid = (1.0 - alpha - beta) * eye - (alpha + 2.0 * beta) * off - beta * square
    gain = 2.0 / (2.0 - spread * spread)
    x = gain * (x + dot1(x.astype(BF16), resid.astype(BF16)))
    spread = spread * spread / (2.0 - spread * spread)
    gain = 2.0 / (2.0 - spread * spread)
    x_high = x.astype(BF16)
    resid = eye - dot1(a_high[...], x_high)
    x_ref[...] = (gain * (x + dot1(x_high, resid.astype(BF16)))).astype(BF16)

    def refine(state):
        step, _ = state
        x = x_ref[...]
        resid = eye - (dot1(a_high[...], x) + dot1(a_low[...], x))
        resid_high = resid.astype(BF16)
        second = dot1(resid_high, resid_high)
        bound = jnp.sum(second * second)
        bound = bound * jnp.sqrt(bound)
        change = halves(resid + second)
        new = x.astype(F32) + (dot1(x, change[0]) + dot1(x, change[1]))
        x_ref[...] = new.astype(BF16)
        inverse_ref[...] = new
        return step + 1, bound

    limit = TOLERANCE * TOLERANCE * size

    def going(state):
        step, bound = state
        return jnp.logical_and(step < MAX_STEPS, bound >= limit)

    _, bound = lax.while_loop(going, refine, refine((jnp.int32(0), jnp.float32(0.0))))
    converged = bound < limit

    @pl.when(jnp.logical_not(converged))
    def _():
        inverse_ref[...] = scaled()

        def eliminate(k, carry):
            block = inverse_ref[...]
            row = inverse_ref[pl.ds(k, 1), :]
            lane = lax.broadcasted_iota(jnp.int32, (1, size), 1) == k
            pivot = jnp.sum(jnp.where(lane, row, 0.0), axis=1, keepdims=True)
            row = jnp.where(lane, 1.0, row) / pivot
            column = jnp.sum(jnp.where(lane, block, 0.0), axis=1, keepdims=True)
            inverse_ref[...] = jnp.where(lane, 0.0, block) - column * row
            inverse_ref[pl.ds(k, 1), :] = row
            return carry

        lax.fori_loop(0, size, eliminate, 0)

    p_ref[...] = inverse_ref[...] * scale_col * scale_row


def invert(diag):
    size = diag.shape[0]
    return pl.pallas_call(
        invert_kernel,
        out_shape=jax.ShapeDtypeStruct((size, size), F32),
        in_specs=[pl.BlockSpec(memory_space=VMEM)],
        out_specs=pl.BlockSpec(memory_space=VMEM),
        scratch_shapes=[
            VMEM((size, size), F32),
            VMEM((size, size), BF16),
            VMEM((size, size), BF16),
            VMEM((size, size), BF16),
        ],
        cost_estimate=pl.CostEstimate(
            flops=24 * size**3, bytes_accessed=8 * size * size, transcendentals=0
        ),
        compiler_params=pltpu.CompilerParams(vmem_limit_bytes=VMEM_LIMIT),
        name="invert_block",
    )(diag)


BLOCK = 128
PACKED = 4 * BLOCK + 8
NEAR = 2 * BLOCK + 8
CHUNKS = ((0, NEAR), (NEAR, 2 * BLOCK))


def block_at(ref, row, col):
    row, col = pl.multiple_of(row * BLOCK, BLOCK), pl.multiple_of(col * BLOCK, BLOCK)
    return ref[pl.ds(row, BLOCK), pl.ds(col, BLOCK)]


def pack_near(ref, first, core, packed):
    own = 2 * core
    packed[:BLOCK] = block_at(ref, first, own + 1)
    rows = lax.broadcasted_iota(jnp.int32, (BLOCK, BLOCK), 0)
    cols = lax.broadcasted_iota(jnp.int32, (BLOCK, BLOCK), 1)
    second = block_at(ref, first + 1, own + 1)
    packed[BLOCK : 2 * BLOCK] = jnp.where(rows >= cols, block_at(ref, first, own), second)
    diagonal = jnp.sum(jnp.where(rows == cols, second, 0.0), axis=0, keepdims=True)
    packed[2 * BLOCK : NEAR] = jnp.broadcast_to(diagonal, (8, BLOCK))


def pack_far(ref, first, core, packed):
    other = 2 - 2 * core
    packed[NEAR : NEAR + BLOCK] = block_at(ref, first + core, other)
    packed[NEAR + BLOCK :] = block_at(ref, first + 1, other + core)


def unpack(shares, full):
    def put(row, col, value):
        full[row * BLOCK : (row + 1) * BLOCK, col * BLOCK : (col + 1) * BLOCK] = value

    rows = lax.broadcasted_iota(jnp.int32, (BLOCK, BLOCK), 0)
    cols = lax.broadcasted_iota(jnp.int32, (BLOCK, BLOCK), 1)
    for core, places in enumerate((((0, 1), (0, 2), (1, 2)), ((2, 3), (3, 0), (3, 1)))):
        for at, (row, col) in zip((0, NEAR, NEAR + BLOCK), places):
            value = shares[core, at : at + BLOCK]
            put(row, col, value)
            put(col, row, value.T)
        both = shares[core, BLOCK : 2 * BLOCK]
        turned = both.T
        diagonal = shares[core, 2 * BLOCK : 2 * BLOCK + 1]
        put(2 * core, 2 * core, jnp.where(rows >= cols, both, turned))
        second = jnp.where(rows < cols, both, jnp.where(rows > cols, turned, diagonal))
        put(2 * core + 1, 2 * core + 1, second)


def level_kernel(stride, last, *refs):
    relay = stride > 1
    p_ref, low_ref, diag_ref, rhs_ref, *refs = refs
    if relay:
        held_ref, diag_out, rhs_out, carried_out, end_out, *refs = refs
    else:
        diag_out, rhs_out, carried_out, *refs = refs
    low_full, p_out, p_in, p_full, t_own, t_out, t_in, t_full, t_rhs_in, rhs_in, *rest = refs
    if relay:
        p_relay, t_relay, rhs_relay, t_rhs_relay, sems = rest
    else:
        (sems,) = rest
    length = lax.axis_size("tm")
    row, core, up, down, sibling = neighbours(1)
    size, width = low_ref.shape
    first = pl.multiple_of(core * width, width)
    mine = pl.ds(first, width)
    has_up = has_above = row + stride < length
    has_down = has_below = row >= stride
    near_up, near_down = row + 1 < length, row >= 1
    between = jnp.logical_and(near_up, near_down)

    barrier = pltpu.get_barrier_semaphore()

    def signal(device):
        pl.semaphore_signal(barrier, inc=1, device_id=device, device_id_type=MESH)

    signal(sibling)
    pl.when(near_up)(lambda: signal(up))
    pl.when(near_down)(lambda: signal(down))
    waits = 1 + near_up.astype(jnp.int32) + near_down.astype(jnp.int32)
    if relay:
        onward = row_at(row, 1) + stride
        has_onward = onward < length
        pl.when(has_below)(lambda: signal((row_at(row - stride, RING - 1), core)))
        waits += has_onward.astype(jnp.int32)
    low_full[:, mine] = low_ref[...]
    pack_near(p_ref, 2 * core, core, p_out)
    pack_far(p_ref, 2 * core, core, p_out)
    pl.semaphore_wait(barrier, waits)

    used = iter(range(sems.shape[1]))

    def copy(src, dst, device):
        at = next(used)
        return pltpu.make_async_remote_copy(
            src_ref=src,
            dst_ref=dst,
            send_sem=sems.at[0, at],
            recv_sem=sems.at[1, at],
            device_id=device,
            device_id_type=MESH,
        )

    def path(src, held, dst, device):
        if not relay:
            return [copy(src, dst, device)]
        return [copy(src, held, device), copy(held, dst, device)]

    def packed_paths(out, held, into, device):
        parts = [pl.ds(at, n) for at, n in CHUNKS]
        return [
            path(out.at[part], relay and held.at[part], into.at[core, part], device)
            for part in parts
        ]

    def packed_across(into):
        parts = [into.at[core, pl.ds(at, n)] for at, n in CHUNKS]
        return [copy(part, part, sibling) for part in parts]

    p_paths = packed_paths(p_out, relay and p_relay, p_in, up)
    t_paths = packed_paths(t_out, relay and t_relay, t_in, down)
    p_paths.append(path(rhs_ref, relay and rhs_relay, rhs_in, up))
    t_paths.append(path(t_own.at[width:], relay and t_rhs_relay, t_rhs_in, down))
    p_across, t_across = packed_across(p_in), packed_across(t_in)
    low_across = copy(low_ref, low_full.at[:, mine], sibling)

    def each(copies, call):
        for one in copies:
            getattr(one, call)()

    low_across.start()
    if relay:
        end_copy = copy(held_ref, end_out, (onward, core))
        pl.when(has_onward)(end_copy.start)
    pl.when(has_up)(lambda: each([way[0] for way in p_paths], "start"))
    own = halves(jnp.concatenate([low_ref[...].T, rhs_ref[...]], axis=0))
    own = halves(dot3(own, halves(p_ref[...])))
    t_own[:, mine] = dot3(own, halves(low_ref[...]))
    pack_near(t_own, 0, core, t_out)
    pl.when(has_down)(t_paths[0][0].start)
    low_across.wait()
    others = pl.ds(pl.multiple_of((1 - core) * width, width), width)
    t_own[:, others] = dot3(own, halves(low_full[:, others]))
    pack_far(t_own, 0, core, t_out)
    pl.when(has_down)(lambda: each([way[0] for way in t_paths[1:]], "start"))
    low = halves(low_full[...])
    if relay:

        @pl.when(between)
        def _():
            for way in p_paths[:2] + t_paths[:1] + p_paths[2:] + t_paths[1:]:
                way[0].wait_recv()
                way[1].start()

    @pl.when(has_below)
    def _():
        for way, across in zip(p_paths, p_across):
            way[-1].wait_recv()
            across.start()
        each(p_across, "wait_recv")

    unpack(p_in, p_full)
    carried = dot3(low, halves(p_full[...]))
    carried_out[...] = carried
    carried = halves(carried)
    from_diag = dot3(carried, low, NT)
    left = diag_ref[...] - jnp.where(has_below, from_diag, 0.0)
    pl.when(has_below)(p_paths[-1][-1].wait_recv)
    from_rhs = dot3(halves(rhs_in[...]), carried, NT)

    @pl.when(has_above)
    def _():
        for way, across in zip(t_paths, t_across):
            way[-1].wait_recv()
            across.start()
        each(t_across, "wait_recv")

    unpack(t_in, t_full)
    if last:
        t_full[...] = left - jnp.where(has_above, t_full[...], 0.0)
        diag_out[...] = t_full[:, mine]
    else:
        diag_out[...] = left - jnp.where(has_above, t_full[...], 0.0)
    pl.when(has_above)(t_paths[-1][-1].wait_recv)
    rhs_out[...] = (
        rhs_ref[...]
        - jnp.where(has_below, from_rhs, 0.0)
        - jnp.where(has_above, t_rhs_in[...], 0.0)
    )
    pl.when(has_up)(lambda: each([way[0] for way in p_paths], "wait_send"))
    pl.when(has_down)(lambda: each([way[0] for way in t_paths], "wait_send"))
    if relay:
        pl.when(between)(lambda: each([way[1] for way in p_paths + t_paths], "wait_send"))
        pl.when(has_below)(end_copy.wait_recv)
        pl.when(has_onward)(end_copy.wait_send)
    pl.when(has_below)(lambda: each(p_across, "wait_send"))
    pl.when(has_above)(lambda: each(t_across, "wait_send"))


def level(stride, last, p, low_cols, diag, rhs, *held):
    size, width = low_cols.shape
    seqs = rhs.shape[0]
    relay = stride > 1
    full = jax.ShapeDtypeStruct((size, size), F32)
    half = jax.ShapeDtypeStruct((size, width), F32)
    share = VMEM((PACKED, BLOCK), F32)
    shares = VMEM((2, PACKED, BLOCK), F32)
    vectors = VMEM((seqs, size), F32)
    relays = [share, share, vectors, vectors]
    copies = 4 * len(CHUNKS) + 3 + (2 * len(CHUNKS) + 3) * relay
    out_shape = [half if last else full, jax.ShapeDtypeStruct((seqs, size), F32), full]
    out_shape += [jax.ShapeDtypeStruct(part.shape, F32) for part in held]
    in_vmem = pl.BlockSpec(memory_space=VMEM)
    return pl.pallas_call(
        functools.partial(level_kernel, stride, last),
        out_shape=out_shape,
        in_specs=[in_vmem] * (4 + len(held)),
        out_specs=[in_vmem] * len(out_shape),
        scratch_shapes=[
            VMEM((size, size), F32),
            share,
            shares,
            VMEM((size, size), F32),
            VMEM((width + seqs, size), F32),
            share,
            shares,
            VMEM((size, size), F32),
            vectors,
            vectors,
            *(relays if relay else ()),
            pltpu.SemaphoreType.DMA((2, copies)),
        ],
        compiler_params=pltpu.CompilerParams(
            collective_id=stride, has_side_effects=True, vmem_limit_bytes=VMEM_LIMIT
        ),
        name="level_%d" % stride,
    )(p, low_cols, diag, rhs, *held)


def coupling(stride, carried_ref, *low_prev):
    carried = halves(carried_ref[...])
    total, at = 0.0, 0
    for part in low_prev:
        rows = part.shape[0]
        total += dot3([half[:, at : at + rows] for half in carried], halves(part[...]))
        at += rows
    return jnp.where(lax.axis_index("tm") >= 2 * stride, -total, 0.0)


def couple_kernel(stride, carried_ref, low_prev_ref, low_out, top_out, end_out):
    low = coupling(stride, carried_ref, low_prev_ref)
    cut = top_out.shape[0]
    low_out[...] = low
    top_out[...] = low[:cut]
    end_out[...] = low[cut:]


def couple(stride, carried, low_prev):
    size, width = low_prev.shape
    part = jax.ShapeDtypeStruct((size // 2, width), F32)
    in_vmem = pl.BlockSpec(memory_space=VMEM)
    return pl.pallas_call(
        functools.partial(couple_kernel, stride),
        out_shape=(jax.ShapeDtypeStruct((size, width), F32), part, part),
        in_specs=[in_vmem] * 2,
        out_specs=[in_vmem] * 3,
        compiler_params=pltpu.CompilerParams(vmem_limit_bytes=VMEM_LIMIT),
        name="couple",
    )(carried, low_prev)


def finish_kernel(
    stride, carried_ref, top_ref, end_ref, diag_ref, rhs_ref, diag_out, low_out, rhs_out
):
    low_out[...] = coupling(stride, carried_ref, top_ref, end_ref)
    diag_out[...] = diag_ref[...]
    rhs_out[...] = rhs_ref[...]


def finish(stride, carried, top, end, diag, rhs):
    half = jax.ShapeDtypeStruct(diag.shape, F32)
    return pl.pallas_call(
        functools.partial(finish_kernel, stride),
        out_shape=(half, half, jax.ShapeDtypeStruct(rhs.shape, F32)),
        in_specs=[pl.BlockSpec(memory_space=VMEM)] * 5,
        out_specs=[pl.BlockSpec(memory_space=VMEM)] * 3,
        compiler_params=pltpu.CompilerParams(vmem_limit_bytes=VMEM_LIMIT),
        name="finish",
    )(carried, top, end, diag, rhs)


def passed_up(array, stride):
    length = lax.axis_size("tm")
    return lax.ppermute(array, "tm", [(i, i + stride) for i in range(length - stride)])


def passed_west(array, stride):
    length = lax.axis_size("tm")
    pairs = [(i, row_at(i, RING - 1)) for i in range(length - stride)]
    return lax.ppermute(array, "tm", pairs)


def per_device(diagonal, lower, rhs):
    low, rhs_rows = lower[0], rhs[0].T
    low_prev = passed_up(low, 1)
    diag = join(diagonal[0])
    diag, rhs_rows, carried = level(1, False, invert(diag), low, diag, rhs_rows)
    low, low_top, low_end = couple(1, carried, low_prev)
    held = passed_west(low_end, 2)
    top = passed_up(low_top, 2)
    diag, rhs_rows, carried, end = level(2, True, invert(diag), low, diag, rhs_rows, held)
    diag, low, rhs_rows = finish(2, carried, top, end, diag, rhs_rows)
    return diag[None], low[None], rhs_rows.T[None]


def solution(mesh):
    placed = (P("tm", None, "state"),) * 3
    return jax.shard_map(
        per_device, mesh=mesh, in_specs=placed, out_specs=placed, check_vma=False
    )
```

```python
import functools

import jax
import jax.numpy as jnp
from jax import lax
from jax.experimental import pallas as pl
from jax.experimental.pallas import tpu as pltpu
from jax.sharding import PartitionSpec as P

MESH = pl.DeviceIdType.MESH
F32 = jnp.float32
BF16 = jnp.bfloat16
VMEM = pltpu.VMEM
VMEM_LIMIT = 24 * 1024 * 1024

NN = (((1,), (0,)), ((), ()))
NT = (((1,), (1,)), ((), ()))
TN = (((0,), (0,)), ((), ()))

TOLERANCE = 5e-5
MAX_STEPS = 20


def halves(x):
    high = x.astype(BF16)
    return high, (x - high.astype(F32)).astype(BF16)


def dot1(a, b, dims=NN):
    return lax.dot_general(a, b, dims, preferred_element_type=F32)


def dot3(a, b, dims=NN):
    return dot1(a[0], b[0], dims) + (dot1(a[0], b[1], dims) + dot1(a[1], b[0], dims))


def neighbours(stride):
    length = lax.axis_size("tm")
    row = lax.axis_index("tm")
    core = lax.axis_index("state")
    up = (lax.rem(row + stride, length), core)
    down = (lax.rem(row + length - stride, length), core)
    return row, core, up, down, (row, 1 - core)


def greet(devices):
    barrier = pltpu.get_barrier_semaphore()
    for device in devices:
        pl.semaphore_signal(barrier, inc=1, device_id=device, device_id_type=MESH)
    pl.semaphore_wait(barrier, len(devices))


def send(src, dst, sems, at, device):
    copy = pltpu.make_async_remote_copy(
        src_ref=src,
        dst_ref=dst,
        send_sem=sems.at[0, at],
        recv_sem=sems.at[1, at],
        device_id=device,
        device_id_type=MESH,
    )
    copy.start()
    return copy


def join_kernel(part_ref, full_ref, sems, local_sem):
    _, core, _, _, sibling = neighbours(1)
    width = part_ref.shape[1]
    mine = full_ref.at[:, pl.ds(pl.multiple_of(core * width, width), width)]
    greet((sibling,))
    across = send(part_ref, mine, sems, 0, sibling)
    local = pltpu.make_async_copy(part_ref, mine, local_sem)
    local.start()
    across.wait()
    local.wait()


def join(part):
    size, width = part.shape
    return pl.pallas_call(
        join_kernel,
        out_shape=jax.ShapeDtypeStruct((size, 2 * width), F32),
        in_specs=[pl.BlockSpec(memory_space=pltpu.HBM)],
        out_specs=pl.BlockSpec(memory_space=VMEM),
        scratch_shapes=[pltpu.SemaphoreType.DMA((2, 1)), pltpu.SemaphoreType.DMA],
        compiler_params=pltpu.CompilerParams(
            collective_id=0, has_side_effects=True, vmem_limit_bytes=VMEM_LIMIT
        ),
        name="join_halves",
    )(part)


def invert_kernel(d_ref, p_ref, inverse_ref, x_ref, a_high, a_low):
    size = d_ref.shape[0]
    rows = lax.broadcasted_iota(jnp.int32, (size, size), 0)
    cols = lax.broadcasted_iota(jnp.int32, (size, size), 1)
    eye = (rows == cols).astype(F32)
    diag = d_ref[...] * eye
    scale_row = lax.rsqrt(jnp.sum(diag, axis=0, keepdims=True))
    scale_col = lax.rsqrt(jnp.sum(diag, axis=1, keepdims=True))

    def scaled():
        return d_ref[...] * scale_col * scale_row

    a = scaled()
    high, low = halves(a)
    a_high[...] = high
    a_low[...] = low
    off = a - eye
    off_high = off.astype(BF16)
    square = dot1(off_high, off_high)
    top = 1.0 + jnp.sqrt(jnp.sqrt(jnp.sum(square * square))) * 1.01
    bottom = top * (1.0 / 12.0)
    ratio = (top - bottom) / (top + bottom)
    spread = ratio * ratio / (2.0 - ratio * ratio)
    half_sum = 0.5 * (top + bottom)
    gain = 2.0 / (2.0 - ratio * ratio)
    alpha = 2.0 * gain / half_sum
    beta = -gain / (half_sum * half_sum)
    x = (alpha + beta) * eye + beta * off
    resid = (1.0 - alpha - beta) * eye - (alpha + 2.0 * beta) * off - beta * square
    gain = 2.0 / (2.0 - spread * spread)
    x = gain * (x + dot1(x.astype(BF16), resid.astype(BF16)))
    spread = spread * spread / (2.0 - spread * spread)
    gain = 2.0 / (2.0 - spread * spread)
    x_high = x.astype(BF16)
    resid = eye - dot1(a_high[...], x_high)
    x_ref[...] = (gain * (x + dot1(x_high, resid.astype(BF16)))).astype(BF16)

    def refine(state):
        step, _ = state
        x = x_ref[...]
        resid = eye - (dot1(a_high[...], x) + dot1(a_low[...], x))
        resid_high = resid.astype(BF16)
        second = dot1(resid_high, resid_high)
        bound = jnp.sum(second * second)
        bound = bound * jnp.sqrt(bound)
        change = halves(resid + second)
        new = x.astype(F32) + (dot1(x, change[0]) + dot1(x, change[1]))
        x_ref[...] = new.astype(BF16)
        inverse_ref[...] = new
        return step + 1, bound

    limit = TOLERANCE * TOLERANCE * size

    def going(state):
        step, bound = state
        return jnp.logical_and(step < MAX_STEPS, bound >= limit)

    _, bound = lax.while_loop(going, refine, refine((jnp.int32(0), jnp.float32(0.0))))
    converged = bound < limit

    @pl.when(jnp.logical_not(converged))
    def _():
        inverse_ref[...] = scaled()

        def eliminate(k, carry):
            block = inverse_ref[...]
            row = inverse_ref[pl.ds(k, 1), :]
            lane = lax.broadcasted_iota(jnp.int32, (1, size), 1) == k
            pivot = jnp.sum(jnp.where(lane, row, 0.0), axis=1, keepdims=True)
            row = jnp.where(lane, 1.0, row) / pivot
            column = jnp.sum(jnp.where(lane, block, 0.0), axis=1, keepdims=True)
            inverse_ref[...] = jnp.where(lane, 0.0, block) - column * row
            inverse_ref[pl.ds(k, 1), :] = row
            return carry

        lax.fori_loop(0, size, eliminate, 0)

    p_ref[...] = inverse_ref[...] * scale_col * scale_row


def invert(diag):
    size = diag.shape[0]
    return pl.pallas_call(
        invert_kernel,
        out_shape=jax.ShapeDtypeStruct((size, size), F32),
        in_specs=[pl.BlockSpec(memory_space=VMEM)],
        out_specs=pl.BlockSpec(memory_space=VMEM),
        scratch_shapes=[
            VMEM((size, size), F32),
            VMEM((size, size), BF16),
            VMEM((size, size), BF16),
            VMEM((size, size), BF16),
        ],
        cost_estimate=pl.CostEstimate(
            flops=24 * size**3, bytes_accessed=8 * size * size, transcendentals=0
        ),
        compiler_params=pltpu.CompilerParams(vmem_limit_bytes=VMEM_LIMIT),
        name="invert_block",
    )(diag)


BLOCK = 128
PACKED = 4 * BLOCK + 8
NEAR = 2 * BLOCK + 8
CHUNKS = ((0, NEAR), (NEAR, 2 * BLOCK))


def block_at(ref, row, col):
    row, col = pl.multiple_of(row * BLOCK, BLOCK), pl.multiple_of(col * BLOCK, BLOCK)
    return ref[pl.ds(row, BLOCK), pl.ds(col, BLOCK)]


def pack_near(ref, first, core, packed):
    own = 2 * core
    packed[:BLOCK] = block_at(ref, first, own + 1)
    rows = lax.broadcasted_iota(jnp.int32, (BLOCK, BLOCK), 0)
    cols = lax.broadcasted_iota(jnp.int32, (BLOCK, BLOCK), 1)
    second = block_at(ref, first + 1, own + 1)
    packed[BLOCK : 2 * BLOCK] = jnp.where(rows >= cols, block_at(ref, first, own), second)
    diagonal = jnp.sum(jnp.where(rows == cols, second, 0.0), axis=0, keepdims=True)
    packed[2 * BLOCK : NEAR] = jnp.broadcast_to(diagonal, (8, BLOCK))


def pack_far(ref, first, core, packed):
    other = 2 - 2 * core
    packed[NEAR : NEAR + BLOCK] = block_at(ref, first + core, other)
    packed[NEAR + BLOCK :] = block_at(ref, first + 1, other + core)


def unpack(shares, full):
    def put(row, col, value):
        full[row * BLOCK : (row + 1) * BLOCK, col * BLOCK : (col + 1) * BLOCK] = value

    rows = lax.broadcasted_iota(jnp.int32, (BLOCK, BLOCK), 0)
    cols = lax.broadcasted_iota(jnp.int32, (BLOCK, BLOCK), 1)
    for core, places in enumerate((((0, 1), (0, 2), (1, 2)), ((2, 3), (3, 0), (3, 1)))):
        for at, (row, col) in zip((0, NEAR, NEAR + BLOCK), places):
            value = shares[core, at : at + BLOCK]
            put(row, col, value)
            put(col, row, value.T)
        both = shares[core, BLOCK : 2 * BLOCK]
        turned = both.T
        diagonal = shares[core, 2 * BLOCK : 2 * BLOCK + 1]
        put(2 * core, 2 * core, jnp.where(rows >= cols, both, turned))
        second = jnp.where(rows < cols, both, jnp.where(rows > cols, turned, diagonal))
        put(2 * core + 1, 2 * core + 1, second)


def level_kernel(
    stride, last, p_ref, low_ref, diag_ref, rhs_ref, diag_out, rhs_out, carried_out,
    low_full, p_out, p_in, p_full, t_own, t_out, t_in, t_full, t_rhs_in, rhs_in, sems,
):
    length = lax.axis_size("tm")
    row, core, up, down, sibling = neighbours(stride)
    size, width = low_ref.shape
    first = pl.multiple_of(core * width, width)
    mine = pl.ds(first, width)
    has_up = has_above = row + stride < length
    has_down = has_below = row >= stride

    barrier = pltpu.get_barrier_semaphore()

    def signal(device):
        pl.semaphore_signal(barrier, inc=1, device_id=device, device_id_type=MESH)

    signal(sibling)
    pl.when(has_up)(lambda: signal(up))
    pl.when(has_down)(lambda: signal(down))
    low_full[:, mine] = low_ref[...]
    pack_near(p_ref, 2 * core, core, p_out)
    pack_far(p_ref, 2 * core, core, p_out)
    pl.semaphore_wait(
        barrier, 1 + has_up.astype(jnp.int32) + has_down.astype(jnp.int32)
    )

    used = iter(range(sems.shape[1]))

    def copy(src, dst, device):
        at = next(used)
        return pltpu.make_async_remote_copy(
            src_ref=src,
            dst_ref=dst,
            send_sem=sems.at[0, at],
            recv_sem=sems.at[1, at],
            device_id=device,
            device_id_type=MESH,
        )

    def packed_copies(out, into, device):
        parts = [pl.ds(at, n) for at, n in CHUNKS]
        return [copy(out.at[part], into.at[core, part], device) for part in parts]

    def packed_across(into):
        parts = [into.at[core, pl.ds(at, n)] for at, n in CHUNKS]
        return [copy(part, part, sibling) for part in parts]

    p_copies = packed_copies(p_out, p_in, up)
    t_copies = packed_copies(t_out, t_in, down)
    rhs_copy = copy(rhs_ref, rhs_in, up)
    t_rhs_copy = copy(t_own.at[width:], t_rhs_in, down)
    p_across, t_across = packed_across(p_in), packed_across(t_in)
    low_across = copy(low_ref, low_full.at[:, mine], sibling)

    def each(copies, call):
        for one in copies:
            getattr(one, call)()

    low_across.start()
    pl.when(has_up)(lambda: each(p_copies + [rhs_copy], "start"))
    own = halves(jnp.concatenate([low_ref[...].T, rhs_ref[...]], axis=0))
    own = halves(dot3(own, halves(p_ref[...])))
    t_own[:, mine] = dot3(own, halves(low_ref[...]))
    pack_near(t_own, 0, core, t_out)
    pl.when(has_down)(t_copies[0].start)
    low_across.wait()
    others = pl.ds(pl.multiple_of((1 - core) * width, width), width)
    t_own[:, others] = dot3(own, halves(low_full[:, others]))
    pack_far(t_own, 0, core, t_out)
    pl.when(has_down)(lambda: each(t_copies[1:] + [t_rhs_copy], "start"))
    low = halves(low_full[...])
    @pl.when(has_below)
    def _():
        for one, across in zip(p_copies, p_across):
            one.wait_recv()
            across.start()
        each(p_across, "wait_recv")

    unpack(p_in, p_full)
    carried = dot3(low, halves(p_full[...]))
    carried_out[...] = carried
    carried = halves(carried)
    from_diag = dot3(carried, low, NT)
    left = diag_ref[...] - jnp.where(has_below, from_diag, 0.0)
    pl.when(has_below)(rhs_copy.wait_recv)
    from_rhs = dot3(halves(rhs_in[...]), carried, NT)

    @pl.when(has_above)
    def _():
        for one, across in zip(t_copies, t_across):
            one.wait_recv()
            across.start()
        each(t_across, "wait_recv")

    unpack(t_in, t_full)
    if last:
        t_full[...] = left - jnp.where(has_above, t_full[...], 0.0)
        diag_out[...] = t_full[:, mine]
    else:
        diag_out[...] = left - jnp.where(has_above, t_full[...], 0.0)
    pl.when(has_above)(t_rhs_copy.wait_recv)
    rhs_out[...] = (
        rhs_ref[...]
        - jnp.where(has_below, from_rhs, 0.0)
        - jnp.where(has_above, t_rhs_in[...], 0.0)
    )
    pl.when(has_up)(lambda: each(p_copies + [rhs_copy], "wait_send"))
    pl.when(has_down)(lambda: each(t_copies + [t_rhs_copy], "wait_send"))
    pl.when(has_below)(lambda: each(p_across, "wait_send"))
    pl.when(has_above)(lambda: each(t_across, "wait_send"))


def level(stride, last, p, low_cols, diag, rhs):
    size, width = low_cols.shape
    seqs = rhs.shape[0]
    full = jax.ShapeDtypeStruct((size, size), F32)
    half = jax.ShapeDtypeStruct((size, width), F32)
    share = VMEM((PACKED, BLOCK), F32)
    shares = VMEM((2, PACKED, BLOCK), F32)
    vectors = VMEM((seqs, size), F32)
    copies = 4 * len(CHUNKS) + 3
    return pl.pallas_call(
        functools.partial(level_kernel, stride, last),
        out_shape=(half if last else full, jax.ShapeDtypeStruct((seqs, size), F32), full),
        in_specs=[pl.BlockSpec(memory_space=VMEM)] * 4,
        out_specs=[pl.BlockSpec(memory_space=VMEM)] * 3,
        scratch_shapes=[
            VMEM((size, size), F32),
            share,
            shares,
            VMEM((size, size), F32),
            VMEM((width + seqs, size), F32),
            share,
            shares,
            VMEM((size, size), F32),
            vectors,
            vectors,
            pltpu.SemaphoreType.DMA((2, copies)),
        ],
        compiler_params=pltpu.CompilerParams(
            collective_id=stride, has_side_effects=True, vmem_limit_bytes=VMEM_LIMIT
        ),
        name="level_%d" % stride,
    )(p, low_cols, diag, rhs)


def couple_kernel(stride, carried_ref, low_prev_ref, low_out):
    product = dot3(halves(carried_ref[...]), halves(low_prev_ref[...]))
    low_out[...] = jnp.where(lax.axis_index("tm") >= 2 * stride, -product, 0.0)


def couple(stride, carried, low_prev):
    return pl.pallas_call(
        functools.partial(couple_kernel, stride),
        out_shape=jax.ShapeDtypeStruct(low_prev.shape, F32),
        in_specs=[pl.BlockSpec(memory_space=VMEM)] * 2,
        out_specs=pl.BlockSpec(memory_space=VMEM),
        compiler_params=pltpu.CompilerParams(vmem_limit_bytes=VMEM_LIMIT),
        name="couple",
    )(carried, low_prev)


def finish_kernel(stride, carried_ref, low_prev_ref, diag_ref, rhs_ref, diag_out, low_out, rhs_out):
    couple_kernel(stride, carried_ref, low_prev_ref, low_out)
    diag_out[...] = diag_ref[...]
    rhs_out[...] = rhs_ref[...]


def finish(stride, carried, low_prev, diag, rhs):
    half = jax.ShapeDtypeStruct(diag.shape, F32)
    return pl.pallas_call(
        functools.partial(finish_kernel, stride),
        out_shape=(half, half, jax.ShapeDtypeStruct(rhs.shape, F32)),
        in_specs=[pl.BlockSpec(memory_space=VMEM)] * 4,
        out_specs=[pl.BlockSpec(memory_space=VMEM)] * 3,
        compiler_params=pltpu.CompilerParams(vmem_limit_bytes=VMEM_LIMIT),
        name="finish",
    )(carried, low_prev, diag, rhs)


def passed_up(array, stride):
    length = lax.axis_size("tm")
    return lax.ppermute(array, "tm", [(i, i + stride) for i in range(length - stride)])


def per_device(diagonal, lower, rhs):
    low_cols, rhs_rows = lower[0], rhs[0].T
    low_prev = passed_up(low_cols, 1)
    diag = join(diagonal[0])
    diag, rhs_rows, carried = level(1, False, invert(diag), low_cols, diag, rhs_rows)
    low_cols = couple(1, carried, low_prev)
    low_prev = passed_up(low_cols, 2)
    diag, rhs_rows, carried = level(2, True, invert(diag), low_cols, diag, rhs_rows)
    diag, low_cols, rhs_rows = finish(2, carried, low_prev, diag, rhs_rows)
    return diag[None], low_cols[None], rhs_rows.T[None]


def solution(mesh):
    placed = (P("tm", None, "state"),) * 3
    return jax.shard_map(
        per_device, mesh=mesh, in_specs=placed, out_specs=placed, check_vma=False
    )
```

```python
import functools

import jax
import jax.numpy as jnp
from jax import lax
from jax.experimental import pallas as pl
from jax.experimental.pallas import tpu as pltpu
from jax.sharding import PartitionSpec as P

MESH = pl.DeviceIdType.MESH
F32 = jnp.float32
BF16 = jnp.bfloat16
VMEM = pltpu.VMEM
VMEM_LIMIT = 24 * 1024 * 1024

NN = (((1,), (0,)), ((), ()))
NT = (((1,), (1,)), ((), ()))
TN = (((0,), (0,)), ((), ()))

TOLERANCE = 5e-5
MAX_STEPS = 20


def halves(x):
    high = x.astype(BF16)
    return high, (x - high.astype(F32)).astype(BF16)


def dot1(a, b, dims=NN):
    return lax.dot_general(a, b, dims, preferred_element_type=F32)


def dot3(a, b, dims=NN):
    return dot1(a[0], b[0], dims) + (dot1(a[0], b[1], dims) + dot1(a[1], b[0], dims))


def neighbours(stride):
    length = lax.axis_size("tm")
    row = lax.axis_index("tm")
    core = lax.axis_index("state")
    up = (lax.rem(row + stride, length), core)
    down = (lax.rem(row + length - stride, length), core)
    return row, core, up, down, (row, 1 - core)


def greet(devices):
    barrier = pltpu.get_barrier_semaphore()
    for device in devices:
        pl.semaphore_signal(barrier, inc=1, device_id=device, device_id_type=MESH)
    pl.semaphore_wait(barrier, len(devices))


def send(src, dst, sems, at, device):
    copy = pltpu.make_async_remote_copy(
        src_ref=src,
        dst_ref=dst,
        send_sem=sems.at[0, at],
        recv_sem=sems.at[1, at],
        device_id=device,
        device_id_type=MESH,
    )
    copy.start()
    return copy


def join_kernel(part_ref, full_ref, sems, local_sem):
    _, core, _, _, sibling = neighbours(1)
    width = part_ref.shape[1]
    mine = full_ref.at[:, pl.ds(pl.multiple_of(core * width, width), width)]
    greet((sibling,))
    across = send(part_ref, mine, sems, 0, sibling)
    local = pltpu.make_async_copy(part_ref, mine, local_sem)
    local.start()
    across.wait()
    local.wait()


def join(part):
    size, width = part.shape
    return pl.pallas_call(
        join_kernel,
        out_shape=jax.ShapeDtypeStruct((size, 2 * width), F32),
        in_specs=[pl.BlockSpec(memory_space=pltpu.HBM)],
        out_specs=pl.BlockSpec(memory_space=VMEM),
        scratch_shapes=[pltpu.SemaphoreType.DMA((2, 1)), pltpu.SemaphoreType.DMA],
        compiler_params=pltpu.CompilerParams(
            collective_id=0, has_side_effects=True, vmem_limit_bytes=VMEM_LIMIT
        ),
        name="join_halves",
    )(part)


def invert_kernel(d_ref, p_ref, inverse_ref, x_ref, a_high, a_low):
    size = d_ref.shape[0]
    rows = lax.broadcasted_iota(jnp.int32, (size, size), 0)
    cols = lax.broadcasted_iota(jnp.int32, (size, size), 1)
    eye = (rows == cols).astype(F32)
    diag = d_ref[...] * eye
    scale_row = lax.rsqrt(jnp.sum(diag, axis=0, keepdims=True))
    scale_col = lax.rsqrt(jnp.sum(diag, axis=1, keepdims=True))

    def scaled():
        return d_ref[...] * scale_col * scale_row

    a = scaled()
    high, low = halves(a)
    a_high[...] = high
    a_low[...] = low
    off = a - eye
    off_high = off.astype(BF16)
    square = dot1(off_high, off_high)
    top = 1.0 + jnp.sqrt(jnp.sqrt(jnp.sum(square * square))) * 1.01
    bottom = top * (1.0 / 12.0)
    ratio = (top - bottom) / (top + bottom)
    spread = ratio * ratio / (2.0 - ratio * ratio)
    half_sum = 0.5 * (top + bottom)
    gain = 2.0 / (2.0 - ratio * ratio)
    alpha = 2.0 * gain / half_sum
    beta = -gain / (half_sum * half_sum)
    x = (alpha + beta) * eye + beta * off
    resid = (1.0 - alpha - beta) * eye - (alpha + 2.0 * beta) * off - beta * square
    gain = 2.0 / (2.0 - spread * spread)
    x = gain * (x + dot1(x.astype(BF16), resid.astype(BF16)))
    spread = spread * spread / (2.0 - spread * spread)
    gain = 2.0 / (2.0 - spread * spread)
    x_high = x.astype(BF16)
    resid = eye - dot1(a_high[...], x_high)
    x_ref[...] = (gain * (x + dot1(x_high, resid.astype(BF16)))).astype(BF16)

    def refine(state):
        step, _ = state
        x = x_ref[...]
        resid = eye - (dot1(a_high[...], x) + dot1(a_low[...], x))
        resid_high = resid.astype(BF16)
        second = dot1(resid_high, resid_high)
        bound = jnp.sum(second * second)
        bound = bound * jnp.sqrt(bound)
        change = halves(resid + second)
        new = x.astype(F32) + (dot1(x, change[0]) + dot1(x, change[1]))
        x_ref[...] = new.astype(BF16)
        inverse_ref[...] = new
        return step + 1, bound

    limit = TOLERANCE * TOLERANCE * size

    def going(state):
        step, bound = state
        return jnp.logical_and(step < MAX_STEPS, bound >= limit)

    _, bound = lax.while_loop(going, refine, refine((jnp.int32(0), jnp.float32(0.0))))
    converged = bound < limit

    @pl.when(jnp.logical_not(converged))
    def _():
        inverse_ref[...] = scaled()

        def eliminate(k, carry):
            block = inverse_ref[...]
            row = inverse_ref[pl.ds(k, 1), :]
            lane = lax.broadcasted_iota(jnp.int32, (1, size), 1) == k
            pivot = jnp.sum(jnp.where(lane, row, 0.0), axis=1, keepdims=True)
            row = jnp.where(lane, 1.0, row) / pivot
            column = jnp.sum(jnp.where(lane, block, 0.0), axis=1, keepdims=True)
            inverse_ref[...] = jnp.where(lane, 0.0, block) - column * row
            inverse_ref[pl.ds(k, 1), :] = row
            return carry

        lax.fori_loop(0, size, eliminate, 0)

    p_ref[...] = inverse_ref[...] * scale_col * scale_row


def invert(diag):
    size = diag.shape[0]
    return pl.pallas_call(
        invert_kernel,
        out_shape=jax.ShapeDtypeStruct((size, size), F32),
        in_specs=[pl.BlockSpec(memory_space=VMEM)],
        out_specs=pl.BlockSpec(memory_space=VMEM),
        scratch_shapes=[
            VMEM((size, size), F32),
            VMEM((size, size), BF16),
            VMEM((size, size), BF16),
            VMEM((size, size), BF16),
        ],
        cost_estimate=pl.CostEstimate(
            flops=24 * size**3, bytes_accessed=8 * size * size, transcendentals=0
        ),
        compiler_params=pltpu.CompilerParams(vmem_limit_bytes=VMEM_LIMIT),
        name="invert_block",
    )(diag)


BLOCK = 128
PACKED = 4 * BLOCK + 8
NEAR = 2 * BLOCK + 8
CHUNKS = ((0, NEAR), (NEAR, 2 * BLOCK))


def block_at(ref, row, col):
    row, col = pl.multiple_of(row * BLOCK, BLOCK), pl.multiple_of(col * BLOCK, BLOCK)
    return ref[pl.ds(row, BLOCK), pl.ds(col, BLOCK)]


def pack_near(ref, first, core, packed):
    own = 2 * core
    packed[:BLOCK] = block_at(ref, first, own + 1)
    rows = lax.broadcasted_iota(jnp.int32, (BLOCK, BLOCK), 0)
    cols = lax.broadcasted_iota(jnp.int32, (BLOCK, BLOCK), 1)
    second = block_at(ref, first + 1, own + 1)
    packed[BLOCK : 2 * BLOCK] = jnp.where(rows >= cols, block_at(ref, first, own), second)
    diagonal = jnp.sum(jnp.where(rows == cols, second, 0.0), axis=0, keepdims=True)
    packed[2 * BLOCK : NEAR] = jnp.broadcast_to(diagonal, (8, BLOCK))


def pack_far(ref, first, core, packed):
    other = 2 - 2 * core
    packed[NEAR : NEAR + BLOCK] = block_at(ref, first + core, other)
    packed[NEAR + BLOCK :] = block_at(ref, first + 1, other + core)


def unpack(shares, full):
    def put(row, col, value):
        full[row * BLOCK : (row + 1) * BLOCK, col * BLOCK : (col + 1) * BLOCK] = value

    rows = lax.broadcasted_iota(jnp.int32, (BLOCK, BLOCK), 0)
    cols = lax.broadcasted_iota(jnp.int32, (BLOCK, BLOCK), 1)
    for core, places in enumerate((((0, 1), (0, 2), (1, 2)), ((2, 3), (3, 0), (3, 1)))):
        for at, (row, col) in zip((0, NEAR, NEAR + BLOCK), places):
            value = shares[core, at : at + BLOCK]
            put(row, col, value)
            put(col, row, value.T)
        both = shares[core, BLOCK : 2 * BLOCK]
        turned = both.T
        diagonal = shares[core, 2 * BLOCK : 2 * BLOCK + 1]
        put(2 * core, 2 * core, jnp.where(rows >= cols, both, turned))
        second = jnp.where(rows < cols, both, jnp.where(rows > cols, turned, diagonal))
        put(2 * core + 1, 2 * core + 1, second)


def level_kernel(stride, last, *refs):
    p_ref, low_ref, diag_ref, rhs_ref, diag_out, rhs_out, carried_out, *refs = refs
    if last:
        low_prev_out, *refs = refs
    low_full, p_out, p_in, p_full, t_own, t_out, t_in, t_full, t_rhs_in, rhs_in, sems = refs
    length = lax.axis_size("tm")
    row, core, up, down, sibling = neighbours(stride)
    size, width = low_ref.shape
    first = pl.multiple_of(core * width, width)
    mine = pl.ds(first, width)
    has_up = has_above = row + stride < length
    has_down = has_below = row >= stride

    barrier = pltpu.get_barrier_semaphore()

    def signal(device):
        pl.semaphore_signal(barrier, inc=1, device_id=device, device_id_type=MESH)

    signal(sibling)
    pl.when(has_up)(lambda: signal(up))
    pl.when(has_down)(lambda: signal(down))
    low_full[:, mine] = low_ref[...]
    pack_near(p_ref, 2 * core, core, p_out)
    pack_far(p_ref, 2 * core, core, p_out)
    pl.semaphore_wait(
        barrier, 1 + has_up.astype(jnp.int32) + has_down.astype(jnp.int32)
    )

    used = iter(range(sems.shape[1]))

    def copy(src, dst, device):
        at = next(used)
        return pltpu.make_async_remote_copy(
            src_ref=src,
            dst_ref=dst,
            send_sem=sems.at[0, at],
            recv_sem=sems.at[1, at],
            device_id=device,
            device_id_type=MESH,
        )

    def packed_copies(out, into, device):
        parts = [pl.ds(at, n) for at, n in CHUNKS]
        return [copy(out.at[part], into.at[core, part], device) for part in parts]

    def packed_across(into):
        parts = [into.at[core, pl.ds(at, n)] for at, n in CHUNKS]
        return [copy(part, part, sibling) for part in parts]

    p_copies = packed_copies(p_out, p_in, up)
    t_copies = packed_copies(t_out, t_in, down)
    rhs_copy = copy(rhs_ref, rhs_in, up)
    t_rhs_copy = copy(t_own.at[width:], t_rhs_in, down)
    p_across, t_across = packed_across(p_in), packed_across(t_in)
    low_across = copy(low_ref, low_full.at[:, mine], sibling)
    if last:
        low_copy = copy(low_ref, low_prev_out, up)

    def each(copies, call):
        for one in copies:
            getattr(one, call)()

    low_across.start()
    pl.when(has_up)(lambda: each(p_copies + [rhs_copy], "start"))
    own = halves(jnp.concatenate([low_ref[...].T, rhs_ref[...]], axis=0))
    own = halves(dot3(own, halves(p_ref[...])))
    t_own[:, mine] = dot3(own, halves(low_ref[...]))
    pack_near(t_own, 0, core, t_out)
    pl.when(has_down)(t_copies[0].start)
    low_across.wait()
    others = pl.ds(pl.multiple_of((1 - core) * width, width), width)
    t_own[:, others] = dot3(own, halves(low_full[:, others]))
    pack_far(t_own, 0, core, t_out)
    pl.when(has_down)(lambda: each(t_copies[1:] + [t_rhs_copy], "start"))
    if last:
        pl.when(has_up)(low_copy.start)
    low = halves(low_full[...])
    @pl.when(has_below)
    def _():
        for one, across in zip(p_copies, p_across):
            one.wait_recv()
            across.start()
        each(p_across, "wait_recv")

    unpack(p_in, p_full)
    carried = dot3(low, halves(p_full[...]))
    carried_out[...] = carried
    carried = halves(carried)
    from_diag = dot3(carried, low, NT)
    left = diag_ref[...] - jnp.where(has_below, from_diag, 0.0)
    pl.when(has_below)(rhs_copy.wait_recv)
    from_rhs = dot3(halves(rhs_in[...]), carried, NT)

    @pl.when(has_above)
    def _():
        for one, across in zip(t_copies, t_across):
            one.wait_recv()
            across.start()
        each(t_across, "wait_recv")

    unpack(t_in, t_full)
    if last:
        t_full[...] = left - jnp.where(has_above, t_full[...], 0.0)
        diag_out[...] = t_full[:, mine]
    else:
        diag_out[...] = left - jnp.where(has_above, t_full[...], 0.0)
    pl.when(has_above)(t_rhs_copy.wait_recv)
    rhs_out[...] = (
        rhs_ref[...]
        - jnp.where(has_below, from_rhs, 0.0)
        - jnp.where(has_above, t_rhs_in[...], 0.0)
    )
    pl.when(has_up)(lambda: each(p_copies + [rhs_copy], "wait_send"))
    pl.when(has_down)(lambda: each(t_copies + [t_rhs_copy], "wait_send"))
    pl.when(has_below)(lambda: each(p_across, "wait_send"))
    pl.when(has_above)(lambda: each(t_across, "wait_send"))
    if last:
        pl.when(has_up)(low_copy.wait_send)
        pl.when(has_below)(low_copy.wait_recv)


def level(stride, last, p, low_cols, diag, rhs):
    size, width = low_cols.shape
    seqs = rhs.shape[0]
    full = jax.ShapeDtypeStruct((size, size), F32)
    half = jax.ShapeDtypeStruct((size, width), F32)
    share = VMEM((PACKED, BLOCK), F32)
    shares = VMEM((2, PACKED, BLOCK), F32)
    vectors = VMEM((seqs, size), F32)
    copies = 4 * len(CHUNKS) + 3 + last
    out_shape = [half if last else full, jax.ShapeDtypeStruct((seqs, size), F32), full]
    if last:
        out_shape.append(half)
    in_vmem = pl.BlockSpec(memory_space=VMEM)
    return pl.pallas_call(
        functools.partial(level_kernel, stride, last),
        out_shape=out_shape,
        in_specs=[in_vmem] * 4,
        out_specs=[in_vmem] * len(out_shape),
        scratch_shapes=[
            VMEM((size, size), F32),
            share,
            shares,
            VMEM((size, size), F32),
            VMEM((width + seqs, size), F32),
            share,
            shares,
            VMEM((size, size), F32),
            vectors,
            vectors,
            pltpu.SemaphoreType.DMA((2, copies)),
        ],
        compiler_params=pltpu.CompilerParams(
            collective_id=stride, has_side_effects=True, vmem_limit_bytes=VMEM_LIMIT
        ),
        name="level_%d" % stride,
    )(p, low_cols, diag, rhs)


def couple_kernel(stride, carried_ref, low_prev_ref, low_out):
    product = dot3(halves(carried_ref[...]), halves(low_prev_ref[...]))
    low_out[...] = jnp.where(lax.axis_index("tm") >= 2 * stride, -product, 0.0)


def couple(stride, carried, low_prev):
    return pl.pallas_call(
        functools.partial(couple_kernel, stride),
        out_shape=jax.ShapeDtypeStruct(low_prev.shape, F32),
        in_specs=[pl.BlockSpec(memory_space=VMEM)] * 2,
        out_specs=pl.BlockSpec(memory_space=VMEM),
        compiler_params=pltpu.CompilerParams(vmem_limit_bytes=VMEM_LIMIT),
        name="couple",
    )(carried, low_prev)


def finish_kernel(stride, carried_ref, low_prev_ref, diag_ref, rhs_ref, diag_out, low_out, rhs_out):
    couple_kernel(stride, carried_ref, low_prev_ref, low_out)
    diag_out[...] = diag_ref[...]
    rhs_out[...] = rhs_ref[...]


def finish(stride, carried, low_prev, diag, rhs):
    half = jax.ShapeDtypeStruct(diag.shape, F32)
    return pl.pallas_call(
        functools.partial(finish_kernel, stride),
        out_shape=(half, half, jax.ShapeDtypeStruct(rhs.shape, F32)),
        in_specs=[pl.BlockSpec(memory_space=VMEM)] * 4,
        out_specs=[pl.BlockSpec(memory_space=VMEM)] * 3,
        compiler_params=pltpu.CompilerParams(vmem_limit_bytes=VMEM_LIMIT),
        name="finish",
    )(carried, low_prev, diag, rhs)


def passed_up(array, stride):
    length = lax.axis_size("tm")
    return lax.ppermute(array, "tm", [(i, i + stride) for i in range(length - stride)])


def per_device(diagonal, lower, rhs):
    low_cols, rhs_rows = lower[0], rhs[0].T
    low_prev = passed_up(low_cols, 1)
    diag = join(diagonal[0])
    diag, rhs_rows, carried = level(1, False, invert(diag), low_cols, diag, rhs_rows)
    low_cols = couple(1, carried, low_prev)
    diag, rhs_rows, carried, low_prev = level(2, True, invert(diag), low_cols, diag, rhs_rows)
    diag, low_cols, rhs_rows = finish(2, carried, low_prev, diag, rhs_rows)
    return diag[None], low_cols[None], rhs_rows.T[None]


def solution(mesh):
    placed = (P("tm", None, "state"),) * 3
    return jax.shard_map(
        per_device, mesh=mesh, in_specs=placed, out_specs=placed, check_vma=False
    )
```

```python
import functools

import jax
import jax.numpy as jnp
from jax import lax
from jax.experimental import pallas as pl
from jax.experimental.pallas import tpu as pltpu
from jax.sharding import PartitionSpec as P

MESH = pl.DeviceIdType.MESH
F32 = jnp.float32
BF16 = jnp.bfloat16
VMEM = pltpu.VMEM
VMEM_LIMIT = 24 * 1024 * 1024

NN = (((1,), (0,)), ((), ()))
NT = (((1,), (1,)), ((), ()))
TN = (((0,), (0,)), ((), ()))

TOLERANCE = 5e-5
MAX_STEPS = 20


def halves(x):
    high = x.astype(BF16)
    return high, (x - high.astype(F32)).astype(BF16)


def dot1(a, b, dims=NN):
    return lax.dot_general(a, b, dims, preferred_element_type=F32)


def dot3(a, b, dims=NN):
    return dot1(a[0], b[0], dims) + (dot1(a[0], b[1], dims) + dot1(a[1], b[0], dims))


RING = 4


def row_at(row, turn):
    return row - row % RING + (row + turn) % RING


def neighbours(stride):
    length = lax.axis_size("tm")
    row = lax.axis_index("tm")
    core = lax.axis_index("state")
    up = (lax.rem(row + stride, length), core)
    down = (lax.rem(row + length - stride, length), core)
    return row, core, up, down, (row, 1 - core)


def greet(devices):
    barrier = pltpu.get_barrier_semaphore()
    for device in devices:
        pl.semaphore_signal(barrier, inc=1, device_id=device, device_id_type=MESH)
    pl.semaphore_wait(barrier, len(devices))


def send(src, dst, sems, at, device):
    copy = pltpu.make_async_remote_copy(
        src_ref=src,
        dst_ref=dst,
        send_sem=sems.at[0, at],
        recv_sem=sems.at[1, at],
        device_id=device,
        device_id_type=MESH,
    )
    copy.start()
    return copy


def join_kernel(part_ref, full_ref, sems, local_sem):
    _, core, _, _, sibling = neighbours(1)
    width = part_ref.shape[1]
    mine = full_ref.at[:, pl.ds(pl.multiple_of(core * width, width), width)]
    greet((sibling,))
    across = send(part_ref, mine, sems, 0, sibling)
    local = pltpu.make_async_copy(part_ref, mine, local_sem)
    local.start()
    across.wait()
    local.wait()


def join(part):
    size, width = part.shape
    return pl.pallas_call(
        join_kernel,
        out_shape=jax.ShapeDtypeStruct((size, 2 * width), F32),
        in_specs=[pl.BlockSpec(memory_space=pltpu.HBM)],
        out_specs=pl.BlockSpec(memory_space=VMEM),
        scratch_shapes=[pltpu.SemaphoreType.DMA((2, 1)), pltpu.SemaphoreType.DMA],
        compiler_params=pltpu.CompilerParams(
            collective_id=0, has_side_effects=True, vmem_limit_bytes=VMEM_LIMIT
        ),
        name="join_halves",
    )(part)


def invert_kernel(d_ref, p_ref, inverse_ref, x_ref, a_high, a_low):
    size = d_ref.shape[0]
    rows = lax.broadcasted_iota(jnp.int32, (size, size), 0)
    cols = lax.broadcasted_iota(jnp.int32, (size, size), 1)
    eye = (rows == cols).astype(F32)
    diag = d_ref[...] * eye
    scale_row = lax.rsqrt(jnp.sum(diag, axis=0, keepdims=True))
    scale_col = lax.rsqrt(jnp.sum(diag, axis=1, keepdims=True))

    def scaled():
        return d_ref[...] * scale_col * scale_row

    a = scaled()
    high, low = halves(a)
    a_high[...] = high
    a_low[...] = low
    off = a - eye
    off_high = off.astype(BF16)
    square = dot1(off_high, off_high)
    top = 1.0 + jnp.sqrt(jnp.sqrt(jnp.sum(square * square))) * 1.01
    bottom = top * (1.0 / 12.0)
    ratio = (top - bottom) / (top + bottom)
    spread = ratio * ratio / (2.0 - ratio * ratio)
    half_sum = 0.5 * (top + bottom)
    gain = 2.0 / (2.0 - ratio * ratio)
    alpha = 2.0 * gain / half_sum
    beta = -gain / (half_sum * half_sum)
    x = (alpha + beta) * eye + beta * off
    resid = (1.0 - alpha - beta) * eye - (alpha + 2.0 * beta) * off - beta * square
    gain = 2.0 / (2.0 - spread * spread)
    x = gain * (x + dot1(x.astype(BF16), resid.astype(BF16)))
    spread = spread * spread / (2.0 - spread * spread)
    gain = 2.0 / (2.0 - spread * spread)
    x_high = x.astype(BF16)
    resid = eye - dot1(a_high[...], x_high)
    x_ref[...] = (gain * (x + dot1(x_high, resid.astype(BF16)))).astype(BF16)

    def refine(state):
        step, _ = state
        x = x_ref[...]
        resid = eye - (dot1(a_high[...], x) + dot1(a_low[...], x))
        resid_high = resid.astype(BF16)
        second = dot1(resid_high, resid_high)
        bound = jnp.sum(second * second)
        bound = bound * jnp.sqrt(bound)
        change = halves(resid + second)
        new = x.astype(F32) + (dot1(x, change[0]) + dot1(x, change[1]))
        x_ref[...] = new.astype(BF16)
        inverse_ref[...] = new
        return step + 1, bound

    limit = TOLERANCE * TOLERANCE * size

    def going(state):
        step, bound = state
        return jnp.logical_and(step < MAX_STEPS, bound >= limit)

    _, bound = lax.while_loop(going, refine, refine((jnp.int32(0), jnp.float32(0.0))))
    converged = bound < limit

    @pl.when(jnp.logical_not(converged))
    def _():
        inverse_ref[...] = scaled()

        def eliminate(k, carry):
            block = inverse_ref[...]
            row = inverse_ref[pl.ds(k, 1), :]
            lane = lax.broadcasted_iota(jnp.int32, (1, size), 1) == k
            pivot = jnp.sum(jnp.where(lane, row, 0.0), axis=1, keepdims=True)
            row = jnp.where(lane, 1.0, row) / pivot
            column = jnp.sum(jnp.where(lane, block, 0.0), axis=1, keepdims=True)
            inverse_ref[...] = jnp.where(lane, 0.0, block) - column * row
            inverse_ref[pl.ds(k, 1), :] = row
            return carry

        lax.fori_loop(0, size, eliminate, 0)

    p_ref[...] = inverse_ref[...] * scale_col * scale_row


def invert(diag):
    size = diag.shape[0]
    return pl.pallas_call(
        invert_kernel,
        out_shape=jax.ShapeDtypeStruct((size, size), F32),
        in_specs=[pl.BlockSpec(memory_space=VMEM)],
        out_specs=pl.BlockSpec(memory_space=VMEM),
        scratch_shapes=[
            VMEM((size, size), F32),
            VMEM((size, size), BF16),
            VMEM((size, size), BF16),
            VMEM((size, size), BF16),
        ],
        cost_estimate=pl.CostEstimate(
            flops=24 * size**3, bytes_accessed=8 * size * size, transcendentals=0
        ),
        compiler_params=pltpu.CompilerParams(vmem_limit_bytes=VMEM_LIMIT),
        name="invert_block",
    )(diag)


BLOCK = 128
PACKED = 4 * BLOCK + 8
NEAR = 2 * BLOCK + 8
CHUNKS = ((0, NEAR), (NEAR, 2 * BLOCK))


def block_at(ref, row, col):
    row, col = pl.multiple_of(row * BLOCK, BLOCK), pl.multiple_of(col * BLOCK, BLOCK)
    return ref[pl.ds(row, BLOCK), pl.ds(col, BLOCK)]


def pack_near(ref, first, core, packed):
    own = 2 * core
    packed[:BLOCK] = block_at(ref, first, own + 1)
    rows = lax.broadcasted_iota(jnp.int32, (BLOCK, BLOCK), 0)
    cols = lax.broadcasted_iota(jnp.int32, (BLOCK, BLOCK), 1)
    second = block_at(ref, first + 1, own + 1)
    packed[BLOCK : 2 * BLOCK] = jnp.where(rows >= cols, block_at(ref, first, own), second)
    diagonal = jnp.sum(jnp.where(rows == cols, second, 0.0), axis=0, keepdims=True)
    packed[2 * BLOCK : NEAR] = jnp.broadcast_to(diagonal, (8, BLOCK))


def pack_far(ref, first, core, packed):
    other = 2 - 2 * core
    packed[NEAR : NEAR + BLOCK] = block_at(ref, first + core, other)
    packed[NEAR + BLOCK :] = block_at(ref, first + 1, other + core)


def unpack(shares, full):
    def put(row, col, value):
        full[row * BLOCK : (row + 1) * BLOCK, col * BLOCK : (col + 1) * BLOCK] = value

    rows = lax.broadcasted_iota(jnp.int32, (BLOCK, BLOCK), 0)
    cols = lax.broadcasted_iota(jnp.int32, (BLOCK, BLOCK), 1)
    for core, places in enumerate((((0, 1), (0, 2), (1, 2)), ((2, 3), (3, 0), (3, 1)))):
        for at, (row, col) in zip((0, NEAR, NEAR + BLOCK), places):
            value = shares[core, at : at + BLOCK]
            put(row, col, value)
            put(col, row, value.T)
        both = shares[core, BLOCK : 2 * BLOCK]
        turned = both.T
        diagonal = shares[core, 2 * BLOCK : 2 * BLOCK + 1]
        put(2 * core, 2 * core, jnp.where(rows >= cols, both, turned))
        second = jnp.where(rows < cols, both, jnp.where(rows > cols, turned, diagonal))
        put(2 * core + 1, 2 * core + 1, second)


def level_kernel(stride, last, *refs):
    p_ref, low_ref, diag_ref, rhs_ref, diag_out, rhs_out, carried_out, *refs = refs
    if last:
        top_out, end_out, held, *refs = refs
    low_full, p_out, p_in, p_full, t_own, t_out, t_in, t_full, t_rhs_in, rhs_in, sems = refs
    length = lax.axis_size("tm")
    row, core, up, down, sibling = neighbours(stride)
    size, width = low_ref.shape
    first = pl.multiple_of(core * width, width)
    mine = pl.ds(first, width)
    has_up = has_above = row + stride < length
    has_down = has_below = row >= stride

    barrier = pltpu.get_barrier_semaphore()

    def signal(device):
        pl.semaphore_signal(barrier, inc=1, device_id=device, device_id_type=MESH)

    signal(sibling)
    pl.when(has_up)(lambda: signal(up))
    pl.when(has_down)(lambda: signal(down))
    waits = 1 + has_up.astype(jnp.int32) + has_down.astype(jnp.int32)
    if last:
        east, west = row_at(row, 1), row_at(row, RING - 1)
        onward = east + stride
        has_onward = onward < length
        pl.when(has_onward)(lambda: signal((east, core)))
        pl.when(has_below)(lambda: signal((row_at(row - stride, RING - 1), core)))
        waits += has_up.astype(jnp.int32) + has_onward.astype(jnp.int32)
    low_full[:, mine] = low_ref[...]
    pack_near(p_ref, 2 * core, core, p_out)
    pack_far(p_ref, 2 * core, core, p_out)
    pl.semaphore_wait(barrier, waits)

    used = iter(range(sems.shape[1]))

    def copy(src, dst, device):
        at = next(used)
        return pltpu.make_async_remote_copy(
            src_ref=src,
            dst_ref=dst,
            send_sem=sems.at[0, at],
            recv_sem=sems.at[1, at],
            device_id=device,
            device_id_type=MESH,
        )

    def packed_copies(out, into, device):
        parts = [pl.ds(at, n) for at, n in CHUNKS]
        return [copy(out.at[part], into.at[core, part], device) for part in parts]

    def packed_across(into):
        parts = [into.at[core, pl.ds(at, n)] for at, n in CHUNKS]
        return [copy(part, part, sibling) for part in parts]

    p_copies = packed_copies(p_out, p_in, up)
    t_copies = packed_copies(t_out, t_in, down)
    rhs_copy = copy(rhs_ref, rhs_in, up)
    t_rhs_copy = copy(t_own.at[width:], t_rhs_in, down)
    p_across, t_across = packed_across(p_in), packed_across(t_in)
    low_across = copy(low_ref, low_full.at[:, mine], sibling)
    if last:
        cut = size // 2
        top_copy = copy(low_ref.at[:cut], top_out, up)
        west_copy = copy(low_ref.at[pl.ds(cut, cut)], held, (west, core))
        end_copy = copy(held, end_out, (onward, core))

    def each(copies, call):
        for one in copies:
            getattr(one, call)()

    low_across.start()
    if last:
        pl.when(has_up)(west_copy.start)
    pl.when(has_up)(lambda: each(p_copies + [rhs_copy], "start"))
    own = halves(jnp.concatenate([low_ref[...].T, rhs_ref[...]], axis=0))
    own = halves(dot3(own, halves(p_ref[...])))
    t_own[:, mine] = dot3(own, halves(low_ref[...]))
    pack_near(t_own, 0, core, t_out)
    pl.when(has_down)(t_copies[0].start)
    low_across.wait()
    others = pl.ds(pl.multiple_of((1 - core) * width, width), width)
    t_own[:, others] = dot3(own, halves(low_full[:, others]))
    pack_far(t_own, 0, core, t_out)
    pl.when(has_down)(lambda: each(t_copies[1:] + [t_rhs_copy], "start"))
    if last:
        pl.when(has_up)(top_copy.start)

        @pl.when(has_onward)
        def _():
            west_copy.wait_recv()
            end_copy.start()

    low = halves(low_full[...])
    @pl.when(has_below)
    def _():
        for one, across in zip(p_copies, p_across):
            one.wait_recv()
            across.start()
        each(p_across, "wait_recv")

    unpack(p_in, p_full)
    carried = dot3(low, halves(p_full[...]))
    carried_out[...] = carried
    carried = halves(carried)
    from_diag = dot3(carried, low, NT)
    left = diag_ref[...] - jnp.where(has_below, from_diag, 0.0)
    pl.when(has_below)(rhs_copy.wait_recv)
    from_rhs = dot3(halves(rhs_in[...]), carried, NT)

    @pl.when(has_above)
    def _():
        for one, across in zip(t_copies, t_across):
            one.wait_recv()
            across.start()
        each(t_across, "wait_recv")

    unpack(t_in, t_full)
    if last:
        t_full[...] = left - jnp.where(has_above, t_full[...], 0.0)
        diag_out[...] = t_full[:, mine]
    else:
        diag_out[...] = left - jnp.where(has_above, t_full[...], 0.0)
    pl.when(has_above)(t_rhs_copy.wait_recv)
    rhs_out[...] = (
        rhs_ref[...]
        - jnp.where(has_below, from_rhs, 0.0)
        - jnp.where(has_above, t_rhs_in[...], 0.0)
    )
    pl.when(has_up)(lambda: each(p_copies + [rhs_copy], "wait_send"))
    pl.when(has_down)(lambda: each(t_copies + [t_rhs_copy], "wait_send"))
    pl.when(has_below)(lambda: each(p_across, "wait_send"))
    pl.when(has_above)(lambda: each(t_across, "wait_send"))
    if last:
        pl.when(has_up)(lambda: each([top_copy, west_copy], "wait_send"))
        pl.when(has_onward)(end_copy.wait_send)
        pl.when(has_below)(lambda: each([top_copy, end_copy], "wait_recv"))


def level(stride, last, p, low_cols, diag, rhs):
    size, width = low_cols.shape
    seqs = rhs.shape[0]
    full = jax.ShapeDtypeStruct((size, size), F32)
    half = jax.ShapeDtypeStruct((size, width), F32)
    share = VMEM((PACKED, BLOCK), F32)
    shares = VMEM((2, PACKED, BLOCK), F32)
    vectors = VMEM((seqs, size), F32)
    copies = 4 * len(CHUNKS) + 3 + 3 * last
    out_shape = [half if last else full, jax.ShapeDtypeStruct((seqs, size), F32), full]
    held = ()
    if last:
        part = (size // 2, width)
        out_shape += [jax.ShapeDtypeStruct(part, F32)] * 2
        held = (VMEM(part, F32),)
    in_vmem = pl.BlockSpec(memory_space=VMEM)
    return pl.pallas_call(
        functools.partial(level_kernel, stride, last),
        out_shape=out_shape,
        in_specs=[in_vmem] * 4,
        out_specs=[in_vmem] * len(out_shape),
        scratch_shapes=[
            *held,
            VMEM((size, size), F32),
            share,
            shares,
            VMEM((size, size), F32),
            VMEM((width + seqs, size), F32),
            share,
            shares,
            VMEM((size, size), F32),
            vectors,
            vectors,
            pltpu.SemaphoreType.DMA((2, copies)),
        ],
        compiler_params=pltpu.CompilerParams(
            collective_id=stride, has_side_effects=True, vmem_limit_bytes=VMEM_LIMIT
        ),
        name="level_%d" % stride,
    )(p, low_cols, diag, rhs)


def coupling(stride, carried_ref, *low_prev):
    carried = halves(carried_ref[...])
    total, at = 0.0, 0
    for part in low_prev:
        rows = part.shape[0]
        total += dot3([half[:, at : at + rows] for half in carried], halves(part[...]))
        at += rows
    return jnp.where(lax.axis_index("tm") >= 2 * stride, -total, 0.0)


def couple_kernel(stride, carried_ref, low_prev_ref, low_out):
    low_out[...] = coupling(stride, carried_ref, low_prev_ref)


def couple(stride, carried, low_prev):
    return pl.pallas_call(
        functools.partial(couple_kernel, stride),
        out_shape=jax.ShapeDtypeStruct(low_prev.shape, F32),
        in_specs=[pl.BlockSpec(memory_space=VMEM)] * 2,
        out_specs=pl.BlockSpec(memory_space=VMEM),
        compiler_params=pltpu.CompilerParams(vmem_limit_bytes=VMEM_LIMIT),
        name="couple",
    )(carried, low_prev)


def finish_kernel(
    stride, carried_ref, top_ref, end_ref, diag_ref, rhs_ref, diag_out, low_out, rhs_out
):
    low_out[...] = coupling(stride, carried_ref, top_ref, end_ref)
    diag_out[...] = diag_ref[...]
    rhs_out[...] = rhs_ref[...]


def finish(stride, carried, top, end, diag, rhs):
    half = jax.ShapeDtypeStruct(diag.shape, F32)
    return pl.pallas_call(
        functools.partial(finish_kernel, stride),
        out_shape=(half, half, jax.ShapeDtypeStruct(rhs.shape, F32)),
        in_specs=[pl.BlockSpec(memory_space=VMEM)] * 5,
        out_specs=[pl.BlockSpec(memory_space=VMEM)] * 3,
        compiler_params=pltpu.CompilerParams(vmem_limit_bytes=VMEM_LIMIT),
        name="finish",
    )(carried, top, end, diag, rhs)


def passed_up(array, stride):
    length = lax.axis_size("tm")
    return lax.ppermute(array, "tm", [(i, i + stride) for i in range(length - stride)])


def per_device(diagonal, lower, rhs):
    low_cols, rhs_rows = lower[0], rhs[0].T
    low_prev = passed_up(low_cols, 1)
    diag = join(diagonal[0])
    diag, rhs_rows, carried = level(1, False, invert(diag), low_cols, diag, rhs_rows)
    low_cols = couple(1, carried, low_prev)
    diag, rhs_rows, carried, *low_prev = level(2, True, invert(diag), low_cols, diag, rhs_rows)
    diag, low_cols, rhs_rows = finish(2, carried, *low_prev, diag, rhs_rows)
    return diag[None], low_cols[None], rhs_rows.T[None]


def solution(mesh):
    placed = (P("tm", None, "state"),) * 3
    return jax.shard_map(
        per_device, mesh=mesh, in_specs=placed, out_specs=placed, check_vma=False
    )
```
